32 devices in a mesh: side: 2 (over core), row: 4 (over y, x), col: 4 (over z).
Axes of the slice: x: 2, y: 2, z: 4, core: 2. Of those that a mesh axis runs over, the one named last changes fastest.
Arguments:
- queries: bfloat16 [512, 128, 576], P(('side', 'row'), 'col'), may hold values from -48 to 48
- cache: bfloat16 [512, 128, 576], P(('side', 'row')), may hold values from -4 to 4
- lengths: int32 [512], P(('side', 'row')), may hold values from 2 to 128, as said below
- w_uv: bfloat16 [128, 512, 128], P('col'), may hold values from -0.25 to 0.25
- w_out: bfloat16 [16384, 7168], P('col', ('side', 'row')), may hold values from -0.046875 to 0.046875
- residual_in: bfloat16 [512, 7168], P('col', ('side', 'row')), may hold values from -8 to 8
- norm_gain: bfloat16 [7168], P(('side', 'row')), may hold values from 0.099609375 to 1.8984375
- expert_ids: int32 [512, 4], P('col'), may hold values from 0 to 7, all different within a row; in each aligned block of 128 rows (0 to 127, 128 to 255, ...) at most 96 rows name the same one
- gate_vals: float32 [512, 4], P('col'), may hold values from 0.05 to 0.5
- w_gate: bfloat16 [8, 7168, 2048], P(('side', 'row'), None, 'col'), may hold values from -0.0625 to 0.0625
- w_up: bfloat16 [8, 7168, 2048], P(('side', 'row'), None, 'col'), may hold values from -0.0625 to 0.0625
- w_down: bfloat16 [8, 2048, 7168], P(('side', 'row'), 'col'), may hold values from -0.125 to 0.125
Outputs:
- mixed: bfloat16 [512, 7168], P('col', ('side', 'row'))
The draws below stay inside these ranges and needn't reach their ends.
Inputs may be any that keep to these rules, and one draw needn't show every extreme that they name: Row b's cache holds its keys in slots below lengths[b]; some row has all 128 slots live. `expert_ids`: each row names 4 different experts; within each aligned block of 128 rows no expert is named by more than 96 rows.
All inputs are finite; a program needn't handle non-finite values.
Results may differ from the reference program's by a relative error of at most 0.015.
Values may be sent and summed in bfloat16 or wider, within the bound.
No kernel may reach another device: no remote copies, remote signals or barrier semaphores. Data moves between devices by JAX's collectives and lax.ppermute only.
A program may use at most 192 MiB of HBM per device.

```python
import math
import jax
import jax.numpy as jnp
import numpy as np
from jax import lax

D = 7168
H = 128
KVL = 512
ROPE = 64
HD = 128
FF = 2048
L = 128
LAT = 576
EXPERTS = 8
TOP = 4
TOKENS = 512
BLOCK = 128
CAPACITY = 96
N_COL = 4


def cache_values(key):
    return jax.random.truncated_normal(key, -4.0, 4.0, (TOKENS, L, LAT), jnp.float32)


def draw_cache(key, part):
    return cache_values(key).astype(jnp.bfloat16)


def draw_queries(key, part):
    key = jax.random.fold_in(key, 11)
    values = jax.random.truncated_normal(key, -4.0, 4.0, (TOKENS, H, LAT), jnp.float32)
    return values.astype(jnp.bfloat16)


def draw_lengths(key, part):
    key = jax.random.fold_in(key, 5)
    values = jax.random.randint(key, (TOKENS,), 2, L + 1)
    first_row = jnp.arange(TOKENS) == 0
    return jnp.where(first_row, L, values).astype(jnp.int32)


def draw_residual_in(key, part):
    key = jax.random.fold_in(key, 7)
    column_pos = jnp.arange(D, dtype=jnp.float32) / D
    column_scale = jnp.exp(jnp.log(0.4) + jnp.log(5.0) * column_pos)
    values = jax.random.truncated_normal(key, -4.0, 4.0, (TOKENS, D), jnp.float32) * column_scale
    return values.astype(jnp.bfloat16)


def block_levels(own_key, shape, split, low, largest):
    factor_of, own = 1.0, jax.random.fold_in(own_key, 6)
    for dim, shards_of in split:
        draws = jnp.exp(jax.random.uniform(jax.random.fold_in(own, dim), (shards_of,), jnp.float32, low / len(split), largest / len(split)))
        factor_of = factor_of * jnp.repeat(draws, shape[dim] // shards_of).reshape([-1 if axis == dim else 1 for axis in range(len(shape))])
    return factor_of


def deal_out(stream_key, own, number, rows, count, top, reach, skew):
    order = jax.random.permutation(stream_key, count)
    crowded, common = load_shares(count, rows * top, reach, skew, True), load_shares(count, rows * top, reach, skew, False)
    places = jnp.arange(count)

    def named(tallies, turn):
        used = int((tallies > 0).sum())
        fixed = max(1, used // 4)
        shifted = fixed + (places - fixed + turn * (used - fixed)) % max(1, count - fixed)
        return jnp.zeros((count,), jnp.int32).at[order[jnp.where(places < fixed, places, shifted)]].set(jnp.asarray(tallies, jnp.int32))

    tallies = jnp.where(number % 4 == 0, named(crowded, number // 4), named(common, number - number // 4 - 1))
    mixed = jax.random.permutation(jax.random.fold_in(own, 3), count)
    giver, receiver = mixed[0:count // 2 * 2:2], mixed[1:count // 2 * 2:2]
    slack = jnp.minimum(tallies[giver] - 1, reach - tallies[receiver]) // 2
    slack = jnp.where((giver == order[0]) | (receiver == order[0]) | (tallies[receiver] == 0), 0, jnp.maximum(slack, 0))
    shifted = jax.random.randint(jax.random.fold_in(own, 4), (count // 2,), 0, 1 << 20) % (slack + 1)
    tallies = tallies.at[giver].add(-shifted).at[receiver].add(shifted)
    labels = jnp.searchsorted(jnp.cumsum(tallies), jnp.arange(rows * top), side="right").astype(jnp.int32)
    listing = labels.reshape(top, rows).T
    listing = listing[jax.random.permutation(jax.random.fold_in(own, 1), rows)]
    turn = jax.random.randint(jax.random.fold_in(own, 2), (rows, 1), 0, top)
    return jnp.take_along_axis(listing, (jnp.arange(top)[None, :] + turn) % top, axis=1)


def load_shares(count, total, limit, slope, full):
    loads = [(1 << 20) // math.isqrt(rank ** slope) + 1 for rank in range(1, count + 1)]
    largest = limit if full else min(limit, max(-(-total // count), total * loads[0] // sum(loads)))
    least = 1 if total - largest >= count - 1 else 0
    holding, spare = [largest] + [least] * (count - 1), total - largest - least * (count - 1)
    while spare > 0:
        movable = [i for i in range(1, count) if holding[i] < largest] or [i for i in range(1, count) if holding[i] < limit]
        pool, budget = sum([loads[i] for i in movable]), spare
        for i in movable:
            extra = min(limit - holding[i], max(1, budget * loads[i] // pool), spare)
            holding[i] = holding[i] + extra
            spare = spare - extra
    return np.array(holding)


def bell_draw(own_key, extent, deviation, limit, cuts=(), held_as=jnp.bfloat16):
    drawn = jax.random.normal(own_key, extent, jnp.float32) * deviation
    if len(cuts) > 0:
        drawn = block_levels(own_key, extent, cuts, -0.22, 0.18) * drawn
    return jnp.clip(drawn, min=-limit, max=limit).astype(held_as)


def setup_inputs(seed: int = 0) -> dict:
    arg_keys = jax.random.split(jax.random.key(seed), 13)
    queries = draw_queries(jax.random.fold_in(arg_keys[12], 71), 0)
    cache = draw_cache(jax.random.fold_in(arg_keys[12], 71), 0)
    lengths = draw_lengths(jax.random.fold_in(arg_keys[12], 71), 0)
    w_uv = bell_draw(arg_keys[3], (H, KVL, HD), KVL ** -0.5, 0.25, ((0, 4),))
    w_out = bell_draw(arg_keys[4], (H * HD, D), (H * HD) ** -0.5, 0.046875, ((0, 4), (1, 8)))
    residual_in = draw_residual_in(jax.random.fold_in(arg_keys[12], 71), 0)
    norm_gain = jnp.clip(1.0 + 0.18 * jax.random.normal(arg_keys[6], (D,), jnp.float32), 0.099609375, 1.8984375).astype(jnp.bfloat16)
    expert_ids_keys = jax.random.split(jax.random.fold_in(arg_keys[7], 1), TOKENS // BLOCK)
    expert_ids_turns = jax.random.permutation(jax.random.fold_in(arg_keys[7], 3), TOKENS // BLOCK)
    expert_ids = jax.vmap(lambda own, number: deal_out(jax.random.fold_in(arg_keys[7], 2), own, number, BLOCK, EXPERTS, TOP, CAPACITY, 1))(expert_ids_keys, expert_ids_turns).reshape((TOKENS, TOP))
    gate_vals = jnp.clip(jnp.exp(math.log(0.5) - 2.3025851 * jax.random.uniform(arg_keys[8], (TOKENS, TOP), jnp.float32) ** block_levels(arg_keys[8], (TOKENS, TOP), ((0, 4),), -0.2, 0.2)), 0.05, 0.5)
    w_gate = bell_draw(arg_keys[9], (EXPERTS, D, FF), D ** -0.5, 0.0625, ((0, 8), (2, 4)))
    w_up = bell_draw(arg_keys[10], (EXPERTS, D, FF), D ** -0.5, 0.0625, ((0, 8), (2, 4)))
    w_down = bell_draw(arg_keys[11], (EXPERTS, FF, D), FF ** -0.5, 0.125, ((0, 8), (1, 4)))
    return dict(queries=queries, cache=cache, lengths=lengths, w_uv=w_uv, w_out=w_out, residual_in=residual_in, norm_gain=norm_gain, expert_ids=expert_ids, gate_vals=gate_vals, w_gate=w_gate, w_up=w_up, w_down=w_down)


def reference(queries, cache, lengths, w_uv, w_out, residual_in, norm_gain, expert_ids, gate_vals, w_gate, w_up, w_down):
    score_scale = (HD + ROPE) ** (-0.5)
    query_wide = queries.astype(jnp.float32)
    cache_wide = cache.astype(jnp.float32)
    scores = jnp.einsum('bhk,blk->bhl', query_wide, cache_wide) * score_scale
    places = jnp.arange(L, dtype=jnp.int32)
    live_mask = places[None, None, :] < lengths[:, None, None]
    scores = jnp.where(live_mask, scores, -jnp.inf)
    row_top = lax.optimization_barrier(jnp.max(scores, axis=2, keepdims=True))
    exp_terms = jnp.exp(scores - row_top)
    attn_probs = (exp_terms / lax.optimization_barrier(jnp.sum(exp_terms, axis=2, keepdims=True))).astype(jnp.bfloat16)
    latent = jnp.einsum('bhl,blk->bhk', attn_probs.astype(jnp.float32), cache_wide[:, :, :KVL]).astype(jnp.bfloat16)
    head_out = jnp.einsum('bhk,hkd->bhd', latent.astype(jnp.float32), w_uv.astype(jnp.float32)).astype(jnp.bfloat16)
    head_out = head_out.reshape(TOKENS, H * HD)
    attention = jnp.dot(head_out, w_out, preferred_element_type=jnp.float32)
    hidden = residual_in.astype(jnp.float32) + attention
    inverse = lax.rsqrt(lax.optimization_barrier(jnp.sum(hidden * hidden, axis=1, keepdims=True)) / D + 1e-06)
    normed = (hidden * inverse * norm_gain.astype(jnp.float32)).astype(jnp.bfloat16)
    part_width = FF // N_COL

    def one_expert(running, items):
        expert_index, gate_mat, up_mat, down_mat = items
        gate_part = jnp.dot(normed, gate_mat, preferred_element_type=jnp.float32)
        up_part = jnp.dot(normed, up_mat, preferred_element_type=jnp.float32)
        activation = (jax.nn.silu(gate_part) * up_part).astype(jnp.bfloat16)
        pieces = jnp.einsum('bpw,pwd->pbd', activation.astype(jnp.float32).reshape(TOKENS, N_COL, part_width), down_mat.astype(jnp.float32).reshape(N_COL, part_width, D))
        rounded = lax.optimization_barrier(pieces.astype(jnp.bfloat16)).astype(jnp.float32)
        expert_rows = lax.optimization_barrier(jnp.sum(rounded, axis=0))
        weight_row = lax.optimization_barrier(jnp.sum(jnp.where(expert_ids == expert_index, gate_vals, 0.0), axis=1))
        return (running + weight_row[:, None] * expert_rows, None)
    start_total = jnp.zeros((TOKENS, D), jnp.float32)
    expert_total, unused = lax.scan(one_expert, start_total, (jnp.arange(EXPERTS, dtype=jnp.int32), w_gate, w_up, w_down))
    return (hidden + expert_total).astype(jnp.bfloat16)
```

```python
import functools

import jax
import jax.numpy as jnp
from jax import lax
from jax.experimental import pallas as pl
from jax.experimental.pallas import tpu as pltpu
from jax.sharding import PartitionSpec as P

ROPE = 64
EPS = 1e-06
MIB = 1024 * 1024
EXTRA = 16
ANY = pl.BlockSpec(memory_space=pl.ANY)
VMEM = pl.BlockSpec(memory_space=pltpu.VMEM)
SMEM = pl.BlockSpec(memory_space=pltpu.SMEM)


def cost(us):
    return pl.CostEstimate(flops=int(us * 1e9), bytes_accessed=1024, transcendentals=0)


LIGHT, STACK, HEAVY = cost(0.001), cost(0.5), cost(100)


def in_hbm(x):
    return pltpu.with_memory_space_constraint(x, pltpu.HBM)


def swap(x, axis, count, d):
    return lax.ppermute(x, axis, [(i, i ^ d) for i in range(count)])


def stack_kernel(n, *refs):
    pieces, (out_ref, held_ref, in_sems, out_sems) = refs[:n], refs[-4:]
    loads, stores, start = [], [], 0
    for i in range(n):
        height = pieces[i].shape[0]
        at = held_ref.at[pl.ds(start, height)]
        loads.append(pltpu.make_async_copy(pieces[i], at, in_sems.at[i]))
        stores.append(
            pltpu.make_async_copy(at, out_ref.at[pl.ds(start, height)], out_sems.at[i])
        )
        start += height
    for load in loads:
        load.start()
    for load, store in zip(loads, stores):
        load.wait()
        store.start()
    for store in stores:
        store.wait()


def stack(pieces, after, estimate=HEAVY):
    n = len(pieces)
    shape = (sum(piece.shape[0] for piece in pieces), pieces[0].shape[1])
    return pl.pallas_call(
        functools.partial(stack_kernel, n),
        in_specs=[ANY] * (n + len(after)),
        out_specs=ANY,
        out_shape=jax.ShapeDtypeStruct(shape, pieces[0].dtype),
        scratch_shapes=[
            pltpu.VMEM(shape, pieces[0].dtype),
            pltpu.SemaphoreType.DMA((n,)),
            pltpu.SemaphoreType.DMA((n,)),
        ],
        compiler_params=pltpu.CompilerParams(vmem_limit_bytes=8 * MIB),
        cost_estimate=estimate,
    )(*pieces, *after)


def hand_on_kernel(x_ref, *refs):
    refs[-1][...] = x_ref[...]


def hand_on(x, after):
    return pl.pallas_call(
        hand_on_kernel,
        in_specs=[VMEM] + [ANY] * len(after),
        out_specs=VMEM,
        out_shape=jax.ShapeDtypeStruct(x.shape, x.dtype),
        compiler_params=pltpu.CompilerParams(vmem_limit_bytes=2 * MIB),
        cost_estimate=HEAVY,
    )(x, *after)


def project_kernel(blocks, n_gate, pos_ref, near_ref, far_ref, w_hbm, *refs):
    outs, (rows_ref, w_ref, acc_ref, sems, w_sems) = refs[-5 - blocks : -5], refs[-5:]
    half, height, full = near_ref.shape
    n = 2 * half
    pieces = [near_ref.at[i] for i in range(half)] + [far_ref.at[i] for i in range(half)]
    copies = [
        pltpu.make_async_copy(
            pieces[i],
            rows_ref.at[pl.ds(pl.multiple_of(pos_ref[i] * height, height), height)],
            sems.at[i],
        )
        for i in range(n)
    ]
    depth = min(512, full)

    def load(k):
        at = pl.ds(pl.multiple_of(k * depth, depth), depth)
        return pltpu.make_async_copy(w_hbm.at[at], w_ref.at[at], w_sems.at[k])

    for copy in copies:
        copy.start()
    for k in range(full // depth):
        load(k).start()
    acc_ref[...] = jnp.zeros_like(acc_ref)
    for copy in copies:
        copy.wait()

    @pl.loop(0, full // depth)
    def _(k):
        load(k).wait()
        at = pl.ds(pl.multiple_of(k * depth, depth), depth)
        acc_ref[...] += jnp.dot(
            rows_ref[:, at], w_ref[at, :], preferred_element_type=jnp.float32
        )

    size = acc_ref.shape[0] // blocks
    for d in range(blocks):
        outs[d][:size, :] = acc_ref[d * size : (d + 1) * size, :].astype(jnp.bfloat16)
    if n_gate:
        gate_ref = refs[0]
        rest, parts = gate_ref[...], []
        for _ in range(3):
            parts.append(rest.astype(jnp.bfloat16).astype(jnp.float32))
            rest = rest - parts[-1]
        parts.append(jnp.zeros((EXTRA - 3, rest.shape[1]), jnp.float32))
        parts = jnp.concatenate(parts, axis=0).astype(jnp.bfloat16)
        for d in range(blocks):
            outs[d][size:, :] = jnp.zeros((EXTRA, outs[d].shape[1]), jnp.bfloat16)
            outs[d][size:, : rest.shape[1]] = parts


def project(near, far, places, w_out, blocks, gate, after):
    half, height, full = near.shape
    n = 2 * half
    width = w_out.shape[1]
    rows = n * height
    held = rows // blocks + EXTRA * len(gate)
    return pl.pallas_call(
        functools.partial(project_kernel, blocks, len(gate)),
        in_specs=[SMEM, ANY, ANY, ANY] + [VMEM] * len(gate) + [ANY] * len(after),
        out_specs=[VMEM] * blocks,
        out_shape=[jax.ShapeDtypeStruct((held, width), jnp.bfloat16)] * blocks,
        scratch_shapes=[
            pltpu.VMEM((rows, full), jnp.bfloat16),
            pltpu.VMEM(w_out.shape, jnp.bfloat16),
            pltpu.VMEM((rows, width), jnp.float32),
            pltpu.SemaphoreType.DMA((n,)),
            pltpu.SemaphoreType.DMA((full // min(512, full),)),
        ],
        compiler_params=pltpu.CompilerParams(vmem_limit_bytes=18 * MIB),
        cost_estimate=HEAVY,
    )(places, near, far, in_hbm(w_out), *gate, *after)


def norm_kernel(chunk, per, n, n_gate, residual_ref, gain_ref, *refs):
    pieces, outs = refs[:n], refs[len(refs) - 2 - n_gate :]
    hidden_ref, scaled_ref = outs[:2]
    rows = hidden_ref.shape[0]
    part = rows // per
    height = residual_ref.shape[0] // per
    for p in range(per):
        to = slice(p * part, (p + 1) * part)
        start = p * height + chunk * part
        hidden = residual_ref[start : start + part, :].astype(jnp.float32)
        for piece in pieces:
            hidden = hidden + piece[to, :].astype(jnp.float32)
        hidden_ref[to, :] = hidden
        scaled_ref[to, :] = (hidden * gain_ref[...].astype(jnp.float32)).astype(jnp.bfloat16)
    if n_gate:
        for d in range(n):
            parts = pieces[d][rows:, : outs[2].shape[1]].astype(jnp.float32)
            outs[2][d : d + 1, :] = parts[0:1] + parts[1:2] + parts[2:3]


def norm(residual, gain, pieces, chunk, per, n_gate, after):
    n = len(pieces)
    block, width = residual.shape
    shape = (pieces[0].shape[0] - EXTRA * n_gate, width)
    return pl.pallas_call(
        functools.partial(norm_kernel, chunk, per, n, n_gate),
        in_specs=[VMEM] * (n + 2) + [ANY] * len(after),
        out_specs=[VMEM] * (2 + n_gate),
        out_shape=[
            jax.ShapeDtypeStruct(shape, jnp.float32),
            jax.ShapeDtypeStruct(shape, jnp.bfloat16),
        ]
        + [jax.ShapeDtypeStruct((n, block), jnp.float32)] * n_gate,
        compiler_params=pltpu.CompilerParams(vmem_limit_bytes=4 * MIB),
        cost_estimate=HEAVY,
    )(residual, gain[None, :], *pieces, *after)


def gate_up_kernel(n_ref, idx_ref, *refs):
    pieces = []
    for ref in refs[:n_ref]:
        pieces += [ref] if len(ref.shape) == 2 else [ref.at[i] for i in range(ref.shape[0])]
    n = len(pieces)
    wg_hbm, wu_hbm, weight_ref = refs[n_ref : n_ref + 3]
    out_ref, x_ref, wg_ref, wu_ref, g_ref, u_ref, sq_ref, sems, wg_sems, wu_sems = refs[-10:]
    width = pieces[0].shape[1]
    rows = out_ref.shape[0]

    def load(i):
        at = pl.ds(pl.multiple_of(idx_ref[i] * width, width), width)
        return (
            pltpu.make_async_copy(wg_hbm.at[at], wg_ref.at[i], wg_sems.at[i]),
            pltpu.make_async_copy(wu_hbm.at[at], wu_ref.at[i], wu_sems.at[i]),
        )

    for i in range(n):
        pltpu.make_async_copy(pieces[i], x_ref.at[i], sems.at[i]).start()
        for copy in load(i):
            copy.start()
    g_ref[...] = jnp.zeros_like(g_ref)
    u_ref[...] = jnp.zeros_like(u_ref)
    sq_ref[...] = jnp.zeros_like(sq_ref)

    @pl.loop(0, n)
    def _(i):
        pltpu.make_async_copy(pieces[0], x_ref.at[i], sems.at[i]).wait()
        x = x_ref[i, :rows, :]
        inverse_gain = 1.0 / x_ref[i, rows:, :][0:1].astype(jnp.float32)
        for copy in load(i):
            copy.wait()
        g_ref[...] += jnp.dot(x, wg_ref[i], preferred_element_type=jnp.float32)
        u_ref[...] += jnp.dot(x, wu_ref[i], preferred_element_type=jnp.float32)
        hidden = x.astype(jnp.float32) * inverse_gain
        sq_ref[...] += jnp.sum(hidden * hidden, axis=1, keepdims=True)

    inv = lax.rsqrt(sq_ref[...] / (n * width) + EPS)
    g = g_ref[...] * inv
    u = u_ref[...] * inv
    out_ref[...] = (g / (1.0 + jnp.exp(-g)) * u * weight_ref[...]).astype(jnp.bfloat16)


def gate_up(pieces, owners, w_gate, w_up, weight):
    n = owners.shape[0]
    held, width = pieces[0].shape[-2:]
    rows = held - EXTRA
    full, units = w_gate.shape
    return pl.pallas_call(
        functools.partial(gate_up_kernel, len(pieces)),
        in_specs=[SMEM] + [ANY] * (len(pieces) + 2) + [VMEM],
        out_specs=VMEM,
        out_shape=jax.ShapeDtypeStruct((rows, units), jnp.bfloat16),
        scratch_shapes=[
            pltpu.VMEM((n, held, width), jnp.bfloat16),
            pltpu.VMEM((n, width, units), jnp.bfloat16),
            pltpu.VMEM((n, width, units), jnp.bfloat16),
            pltpu.VMEM((rows, units), jnp.float32),
            pltpu.VMEM((rows, units), jnp.float32),
            pltpu.VMEM((rows, 1), jnp.float32),
            pltpu.SemaphoreType.DMA((n,)),
            pltpu.SemaphoreType.DMA((n,)),
            pltpu.SemaphoreType.DMA((n,)),
        ],
        compiler_params=pltpu.CompilerParams(vmem_limit_bytes=30 * MIB),
        cost_estimate=HEAVY,
    )(owners, *pieces, in_hbm(w_gate), in_hbm(w_up), weight)


def down_kernel(idx_ref, act_ref, w_ref, out_ref):
    m, _, width = out_ref.shape

    @pl.loop(0, m)
    def _(j):
        at = pl.ds(pl.multiple_of(idx_ref[j] * width, 128), width)
        out_ref[j] = jnp.dot(
            act_ref[...], w_ref[:, at], preferred_element_type=jnp.float32
        ).astype(jnp.bfloat16)


def down(act, owners, w_down, width):
    rows, units = act.shape
    m = owners.shape[0]
    if width % 128:
        cut = [
            lax.dynamic_slice_in_dim(w_down, owners[j] * width, width, axis=1) for j in range(m)
        ]
        return jnp.stack(
            [jnp.dot(act, w, preferred_element_type=jnp.float32).astype(jnp.bfloat16) for w in cut]
        )
    return pl.pallas_call(
        down_kernel,
        in_specs=[SMEM, VMEM, VMEM],
        out_specs=VMEM,
        out_shape=jax.ShapeDtypeStruct((m, rows, width), jnp.bfloat16),
        compiler_params=pltpu.CompilerParams(vmem_limit_bytes=8 * MIB),
        cost_estimate=HEAVY,
    )(owners, act, w_down)


def combine_kernel(n, near_ref, got_ref, *refs):
    outs = refs
    for d in range(n):
        both = near_ref[d].astype(jnp.float32) + got_ref[d].astype(jnp.float32)
        outs[d][...] = both.astype(outs[d].dtype)


def combine(near, got):
    n, rows, width = near.shape
    return pl.pallas_call(
        functools.partial(combine_kernel, n),
        in_specs=[VMEM] * 2,
        out_specs=[VMEM] * n,
        out_shape=[
            jax.ShapeDtypeStruct((rows, width), jnp.bfloat16 if d else jnp.float32)
            for d in range(n)
        ],
        compiler_params=pltpu.CompilerParams(vmem_limit_bytes=12 * MIB),
        cost_estimate=HEAVY,
    )(near, got)


def reduce_kernel(n, blocks, *refs):
    pieces, outs = refs[:n], refs[-blocks:]
    size = outs[0].shape[0]
    for b in range(blocks):
        at = slice(b * size, (b + 1) * size)
        total = pieces[0][at, :]
        for piece in pieces[1:]:
            total = total + piece[at, :].astype(jnp.float32)
        outs[b][...] = total.astype(outs[b].dtype)


def reduce(pieces, blocks, after):
    n = len(pieces)
    rows, width = pieces[0].shape
    return pl.pallas_call(
        functools.partial(reduce_kernel, n, blocks),
        in_specs=[VMEM] * n + [ANY] * len(after),
        out_specs=[VMEM] * blocks,
        out_shape=[
            jax.ShapeDtypeStruct((rows // blocks, width), jnp.bfloat16 if b else jnp.float32)
            for b in range(blocks)
        ],
        compiler_params=pltpu.CompilerParams(vmem_limit_bytes=8 * MIB),
        cost_estimate=HEAVY,
    )(*pieces, *after)


def finish_kernel(chunks, per, n, *refs):
    out_ref = refs[-1]
    part = out_ref.shape[0] // (chunks * per)
    for c in range(chunks):
        pieces = refs[c * n : (c + 1) * n]
        for p in range(per):
            at = slice(p * part, (p + 1) * part)
            total = pieces[0][at, :]
            for piece in pieces[1:]:
                total = total + piece[at, :].astype(jnp.float32)
            start = (p * chunks + c) * part
            out_ref[start : start + part, :] = total.astype(jnp.bfloat16)


def finish(terms, per):
    chunks, n = len(terms), len(terms[0])
    rows, width = terms[0][0].shape
    return pl.pallas_call(
        functools.partial(finish_kernel, chunks, per, n),
        in_specs=[VMEM] * (chunks * n),
        out_specs=VMEM,
        out_shape=jax.ShapeDtypeStruct((chunks * rows, width), jnp.bfloat16),
        compiler_params=pltpu.CompilerParams(vmem_limit_bytes=8 * MIB),
        cost_estimate=HEAVY,
    )(*[x for chunk in terms for x in chunk])


def attend_kernel(scale, chunk, len_ref, q_ref, c_ref, w_hbm, *refs):
    out_ref, w_ref, score_ref, prob_ref, lat_ref, sem = refs[-6:]
    step, steps = pl.program_id(0), pl.num_programs(0)
    group, heads, _ = q_ref.shape
    slots = c_ref.shape[2]
    _, latent_width, size = w_ref.shape
    load = pltpu.make_async_copy(w_hbm, w_ref, sem)

    @pl.when(step == 0)
    def _():
        load.start()

    places = lax.broadcasted_iota(jnp.int32, (heads, slots), 1)
    for r in range(group):
        scores = jnp.dot(q_ref[r], c_ref[r], preferred_element_type=jnp.float32) * scale
        live = len_ref[(chunk * steps + step) * group + r]
        score_ref[r * heads : (r + 1) * heads, :] = jnp.where(places < live, scores, -jnp.inf)
    scores = score_ref[...]
    exp_terms = jnp.exp(scores - jnp.max(scores, axis=1, keepdims=True))
    probs = exp_terms / jnp.sum(exp_terms, axis=1, keepdims=True)
    prob_ref[...] = probs.astype(jnp.bfloat16)
    for r in range(group):
        latent = lax.dot_general(
            prob_ref[r * heads : (r + 1) * heads, :],
            c_ref[r, :latent_width, :],
            (((1,), (1,)), ((), ())),
            preferred_element_type=jnp.float32,
        )
        at = pl.ds(pl.multiple_of((step * group + r) * heads, heads), heads)
        for k in range(latent_width // 128):
            lat_ref[k, at, :] = latent[:, k * 128 : (k + 1) * 128]

    @pl.when(step == steps - 1)
    def _():
        load.wait()
        for h in range(heads):
            at = pl.ds(h, out_ref.shape[0], stride=heads)
            latent = jnp.concatenate(
                [lat_ref[k, at, :] for k in range(latent_width // 128)], axis=1
            ).astype(jnp.bfloat16)
            out_ref[:, h * size : (h + 1) * size] = jnp.dot(
                latent, w_ref[h], preferred_element_type=jnp.float32
            ).astype(jnp.bfloat16)


def attend(queries, cache, lengths, w_uv, chunk, chunks, after):
    rows, heads, entries = queries.shape
    slots = cache.shape[1]
    _, latent_width, size = w_uv.shape
    group = 16
    steps = rows // chunks // group
    return pl.pallas_call(
        functools.partial(attend_kernel, (size + ROPE) ** (-0.5), chunk),
        grid_spec=pltpu.PrefetchScalarGridSpec(
            num_scalar_prefetch=1,
            grid=(steps,),
            in_specs=[
                pl.BlockSpec((group, heads, entries), lambda i, _: (chunk * steps + i, 0, 0)),
                pl.BlockSpec((group, entries, slots), lambda i, _: (chunk * steps + i, 0, 0)),
                ANY,
            ]
            + [ANY] * len(after),
            out_specs=pl.BlockSpec((steps * group, heads * size), lambda i, _: (0, 0)),
            scratch_shapes=[
                pltpu.VMEM(w_uv.shape, jnp.bfloat16),
                pltpu.VMEM((group * heads, slots), jnp.float32),
                pltpu.VMEM((group * heads, slots), jnp.bfloat16),
                pltpu.VMEM((latent_width // 128, steps * group * heads, 128), jnp.float32),
                pltpu.SemaphoreType.DMA,
            ],
        ),
        out_shape=jax.ShapeDtypeStruct((steps * group, heads * size), jnp.bfloat16),
        compiler_params=pltpu.CompilerParams(vmem_limit_bytes=20 * MIB),
        cost_estimate=HEAVY,
    )(
        lengths,
        in_hbm(queries),
        in_hbm(jnp.swapaxes(cache, 1, 2)),
        in_hbm(w_uv),
        *after,
    )


def shards(
    n_row,
    n_col,
    queries,
    cache,
    lengths,
    w_uv,
    w_out,
    residual_in,
    norm_gain,
    expert_ids,
    gate_vals,
    w_gate,
    w_up,
    w_down,
):
    side, row, col = lax.axis_index("side"), lax.axis_index("row"), lax.axis_index("col")
    block, width = residual_in.shape
    height = queries.shape[0]
    per = block // height
    chunks = 2
    part = height // chunks
    owners = jnp.stack(
        [(side ^ ds) * n_row + (row ^ d) for ds in range(2) for d in range(n_row)]
    ).astype(jnp.int32)
    places = (((owners // per) ^ col) * per + owners % per).astype(jnp.int32)

    chosen = expert_ids == owners[0]
    my_gate = jnp.sum(jnp.where(chosen, gate_vals, 0.0), axis=1)[None, :]
    gain = jnp.broadcast_to(norm_gain, (EXTRA, width))

    first = attend(queries, cache, lengths, w_uv, 0, chunks, [])
    second = attend(queries, cache, lengths, w_uv, 1, chunks, [first])
    gate_dev, up_dev, down_dev = w_gate[0], w_up[0], w_down[0]

    def over_col(pieces):
        return [pieces[0]] + [swap(pieces[d], "col", n_col, d) for d in range(1, n_col)]

    def over_row(pieces):
        return [pieces[0]] + [swap(pieces[d], "row", n_row, d) for d in range(1, n_row)]

    def other_core(x):
        return swap(x, "side", 2, 1)

    def experts(near, held):
        far = [other_core(piece) for piece in near]
        act = gate_up(near + far, owners, gate_dev, up_dev, held)
        far_rows = down(act, owners[n_row:], down_dev, width)
        near_rows = down(act, owners[:n_row], down_dev, width)
        return combine(near_rows, other_core(far_rows))

    def stack_rows(x, after, estimate=HEAVY):
        return stack(over_row([x] * n_row), after, estimate).reshape(n_row, *x.shape)

    near_0 = stack_rows(first, [second], STACK)
    partial_0 = project(near_0, other_core(near_0), places, w_out, n_col, [], [])
    near_1 = stack_rows(second, partial_0[:1], STACK)
    hidden_0, scaled_0 = norm(residual_in, norm_gain, over_col(partial_0), 0, per, 0, [])
    partial_1 = project(near_1, other_core(near_1), places, w_out, n_col, [my_gate], [scaled_0])
    rows_0 = stack(over_col([scaled_0] * n_col) + [gain], partial_1[:1])
    hidden_1, scaled_1, gates = norm(
        residual_in, norm_gain, over_col(partial_1), 1, per, 1, [rows_0]
    )
    weight = gates.reshape(n_col, per, chunks, part)
    weight = [weight[:, :, c].reshape(-1, 1) for c in range(chunks)]
    near_0 = over_row([rows_0] * n_row)
    both_0 = experts(near_0, weight[0])
    rows_1 = stack(over_col([scaled_1] * n_col) + [gain], near_0[1:])
    near_1 = stack_rows(rows_1, both_0[:1])
    both_1 = experts([near_1], hand_on(weight[1], [near_1]))
    total_0 = reduce(over_row(both_0), n_col, both_1[:1])
    total_1 = reduce(over_row(both_1), n_col, [])
    terms = [[hidden_0, *over_col(total_0)], [hidden_1, *over_col(total_1)]]
    return finish(terms, per)


def solution(mesh):
    placed = (
        P(("side", "row"), "col", None),
        P(("side", "row"), None, None),
        P(("side", "row")),
        P("col", None, None),
        P("col", ("side", "row")),
        P("col", ("side", "row")),
        P(("side", "row")),
        P("col", None),
        P("col", None),
        P(("side", "row"), None, "col"),
        P(("side", "row"), None, "col"),
        P(("side", "row"), "col", None),
    )
    return jax.shard_map(
        functools.partial(shards, mesh.shape["row"], mesh.shape["col"]),
        mesh=mesh,
        in_specs=placed,
        out_specs=P("col", ("side", "row")),
        check_vma=False,
    )
```

```python
import functools

import jax
import jax.numpy as jnp
from jax import lax
from jax.experimental import pallas as pl
from jax.experimental.pallas import tpu as pltpu
from jax.sharding import PartitionSpec as P

ROPE = 64
EPS = 1e-06
MIB = 1024 * 1024
EXTRA = 16
ANY = pl.BlockSpec(memory_space=pl.ANY)
VMEM = pl.BlockSpec(memory_space=pltpu.VMEM)
SMEM = pl.BlockSpec(memory_space=pltpu.SMEM)


def cost(us):
    return pl.CostEstimate(flops=int(us * 1e9), bytes_accessed=1024, transcendentals=0)


LIGHT, STACK, HEAVY = cost(0.001), cost(0.5), cost(100)


def in_hbm(x):
    return pltpu.with_memory_space_constraint(x, pltpu.HBM)


def swap(x, axis, count, d):
    return lax.ppermute(x, axis, [(i, i ^ d) for i in range(count)])


def stack_kernel(n, *refs):
    pieces, (out_ref, held_ref, in_sems, out_sems) = refs[:n], refs[-4:]
    loads, stores, start = [], [], 0
    for i in range(n):
        height = pieces[i].shape[0]
        at = held_ref.at[pl.ds(start, height)]
        loads.append(pltpu.make_async_copy(pieces[i], at, in_sems.at[i]))
        stores.append(
            pltpu.make_async_copy(at, out_ref.at[pl.ds(start, height)], out_sems.at[i])
        )
        start += height
    for load in loads:
        load.start()
    for load, store in zip(loads, stores):
        load.wait()
        store.start()
    for store in stores:
        store.wait()


def stack(pieces, after, estimate=HEAVY):
    n = len(pieces)
    shape = (sum(piece.shape[0] for piece in pieces), pieces[0].shape[1])
    return pl.pallas_call(
        functools.partial(stack_kernel, n),
        in_specs=[ANY] * (n + len(after)),
        out_specs=ANY,
        out_shape=jax.ShapeDtypeStruct(shape, pieces[0].dtype),
        scratch_shapes=[
            pltpu.VMEM(shape, pieces[0].dtype),
            pltpu.SemaphoreType.DMA((n,)),
            pltpu.SemaphoreType.DMA((n,)),
        ],
        compiler_params=pltpu.CompilerParams(vmem_limit_bytes=8 * MIB),
        cost_estimate=estimate,
    )(*pieces, *after)


def hand_on_kernel(x_ref, *refs):
    refs[-1][...] = x_ref[...]


def hand_on(x, after):
    return pl.pallas_call(
        hand_on_kernel,
        in_specs=[VMEM] + [ANY] * len(after),
        out_specs=VMEM,
        out_shape=jax.ShapeDtypeStruct(x.shape, x.dtype),
        compiler_params=pltpu.CompilerParams(vmem_limit_bytes=2 * MIB),
        cost_estimate=HEAVY,
    )(x, *after)


def project_kernel(blocks, n_gate, pos_ref, near_ref, far_ref, w_hbm, *refs):
    outs, (rows_ref, w_ref, acc_ref, sems, w_sems) = refs[-5 - blocks : -5], refs[-5:]
    half, height, full = near_ref.shape
    n = 2 * half
    pieces = [near_ref.at[i] for i in range(half)] + [far_ref.at[i] for i in range(half)]
    copies = [
        pltpu.make_async_copy(
            pieces[i],
            rows_ref.at[pl.ds(pl.multiple_of(pos_ref[i] * height, height), height)],
            sems.at[i],
        )
        for i in range(n)
    ]
    depth = min(512, full)

    def load(k):
        at = pl.ds(pl.multiple_of(k * depth, depth), depth)
        return pltpu.make_async_copy(w_hbm.at[at], w_ref.at[at], w_sems.at[k])

    for copy in copies:
        copy.start()
    for k in range(full // depth):
        load(k).start()
    acc_ref[...] = jnp.zeros_like(acc_ref)
    for copy in copies:
        copy.wait()

    @pl.loop(0, full // depth)
    def _(k):
        load(k).wait()
        at = pl.ds(pl.multiple_of(k * depth, depth), depth)
        acc_ref[...] += jnp.dot(
            rows_ref[:, at], w_ref[at, :], preferred_element_type=jnp.float32
        )

    size = acc_ref.shape[0] // blocks
    for d in range(blocks):
        outs[d][:size, :] = acc_ref[d * size : (d + 1) * size, :].astype(jnp.bfloat16)
    if n_gate:
        gate_ref = refs[0]
        rest, parts = gate_ref[...], []
        for _ in range(3):
            parts.append(rest.astype(jnp.bfloat16).astype(jnp.float32))
            rest = rest - parts[-1]
        parts.append(jnp.zeros((EXTRA - 3, rest.shape[1]), jnp.float32))
        parts = jnp.concatenate(parts, axis=0).astype(jnp.bfloat16)
        for d in range(blocks):
            outs[d][size:, :] = jnp.zeros((EXTRA, outs[d].shape[1]), jnp.bfloat16)
            outs[d][size:, : rest.shape[1]] = parts


def project(near, far, places, w_out, blocks, gate, after):
    half, height, full = near.shape
    n = 2 * half
    width = w_out.shape[1]
    rows = n * height
    held = rows // blocks + EXTRA * len(gate)
    return pl.pallas_call(
        functools.partial(project_kernel, blocks, len(gate)),
        in_specs=[SMEM, ANY, ANY, ANY] + [VMEM] * len(gate) + [ANY] * len(after),
        out_specs=[VMEM] * blocks,
        out_shape=[jax.ShapeDtypeStruct((held, width), jnp.bfloat16)] * blocks,
        scratch_shapes=[
            pltpu.VMEM((rows, full), jnp.bfloat16),
            pltpu.VMEM(w_out.shape, jnp.bfloat16),
            pltpu.VMEM((rows, width), jnp.float32),
            pltpu.SemaphoreType.DMA((n,)),
            pltpu.SemaphoreType.DMA((full // min(512, full),)),
        ],
        compiler_params=pltpu.CompilerParams(vmem_limit_bytes=18 * MIB),
        cost_estimate=HEAVY,
    )(places, near, far, in_hbm(w_out), *gate, *after)


def norm_kernel(chunk, per, n, n_gate, residual_ref, gain_ref, *refs):
    pieces, outs = refs[:n], refs[len(refs) - 2 - n_gate :]
    hidden_ref, scaled_ref = outs[:2]
    rows = hidden_ref.shape[0]
    part = rows // per
    height = residual_ref.shape[0] // per
    for p in range(per):
        to = slice(p * part, (p + 1) * part)
        start = p * height + chunk * part
        hidden = residual_ref[start : start + part, :].astype(jnp.float32)
        for piece in pieces:
            hidden = hidden + piece[to, :].astype(jnp.float32)
        hidden_ref[to, :] = hidden
        scaled_ref[to, :] = (hidden * gain_ref[...].astype(jnp.float32)).astype(jnp.bfloat16)
    if n_gate:
        for d in range(n):
            parts = pieces[d][rows:, : outs[2].shape[1]].astype(jnp.float32)
            outs[2][d : d + 1, :] = parts[0:1] + parts[1:2] + parts[2:3]


def norm(residual, gain, pieces, chunk, per, n_gate, after):
    n = len(pieces)
    block, width = residual.shape
    shape = (pieces[0].shape[0] - EXTRA * n_gate, width)
    return pl.pallas_call(
        functools.partial(norm_kernel, chunk, per, n, n_gate),
        in_specs=[VMEM] * (n + 2) + [ANY] * len(after),
        out_specs=[VMEM] * (2 + n_gate),
        out_shape=[
            jax.ShapeDtypeStruct(shape, jnp.float32),
            jax.ShapeDtypeStruct(shape, jnp.bfloat16),
        ]
        + [jax.ShapeDtypeStruct((n, block), jnp.float32)] * n_gate,
        compiler_params=pltpu.CompilerParams(vmem_limit_bytes=4 * MIB),
        cost_estimate=HEAVY,
    )(residual, gain[None, :], *pieces, *after)


def gate_up_kernel(n_ref, idx_ref, *refs):
    pieces = []
    for ref in refs[:n_ref]:
        pieces += [ref] if len(ref.shape) == 2 else [ref.at[i] for i in range(ref.shape[0])]
    n = len(pieces)
    wg_hbm, wu_hbm, weight_ref, gain_in = refs[n_ref : n_ref + 4]
    out_ref, gain_ref, x_ref, wg_ref, wu_ref, g_ref, u_ref, sq_ref, sems, wg_sems, wu_sems = refs[-11:]
    width = pieces[0].shape[1]
    rows = out_ref.shape[0]
    group = n // x_ref.shape[0]

    def load(i, j):
        at = pl.ds(pl.multiple_of(idx_ref[i * group + j] * width, width), width)
        to = pl.ds(j * width, width)
        return (
            pltpu.make_async_copy(pieces[0], x_ref.at[i, :, to], sems.at[i * group + j]),
            pltpu.make_async_copy(wg_hbm.at[at], wg_ref.at[i, to], wg_sems.at[i * group + j]),
            pltpu.make_async_copy(wu_hbm.at[at], wu_ref.at[i, to], wu_sems.at[i * group + j]),
        )

    for i in range(n):
        to = x_ref.at[i // group, :, pl.ds(i % group * width, width)]
        pltpu.make_async_copy(pieces[i], to, sems.at[i]).start()
        for copy in load(i // group, i % group)[1:]:
            copy.start()
    g_ref[...] = jnp.zeros_like(g_ref)
    u_ref[...] = jnp.zeros_like(u_ref)
    sq_ref[...] = jnp.zeros_like(sq_ref)
    gain_ref[...] = gain_in[...]

    @pl.loop(0, n // group)
    def _(i):
        for j in range(group):
            for copy in load(i, j):
                copy.wait()
        x = x_ref[i, :rows, :]
        if x_ref.shape[1] > rows:
            gain_ref[pl.ds(i, 1), :] = 1.0 / x_ref[i, rows:, :][0:1].astype(jnp.float32)
        g_ref[...] += jnp.dot(x, wg_ref[i], preferred_element_type=jnp.float32)
        u_ref[...] += jnp.dot(x, wu_ref[i], preferred_element_type=jnp.float32)
        hidden = x.astype(jnp.float32) * gain_ref[pl.ds(i, 1), :]
        sq_ref[...] += jnp.sum(hidden * hidden, axis=1, keepdims=True)

    inv = lax.rsqrt(sq_ref[...] / (n * width) + EPS)
    g = g_ref[...] * inv
    u = u_ref[...] * inv
    out_ref[...] = (g / (1.0 + jnp.exp(-g)) * u * weight_ref[...]).astype(jnp.bfloat16)


def gate_up(pieces, owners, w_gate, w_up, weight, gain):
    n = owners.shape[0]
    held, width = pieces[0].shape[-2:]
    rows = weight.shape[0]
    full, units = w_gate.shape
    group = 2 if width % 128 == 0 else 1
    groups, wide = n // group, group * width
    return pl.pallas_call(
        functools.partial(gate_up_kernel, len(pieces)),
        in_specs=[SMEM] + [ANY] * (len(pieces) + 2) + [VMEM] * 2,
        out_specs=[VMEM] * 2,
        out_shape=[
            jax.ShapeDtypeStruct((rows, units), jnp.bfloat16),
            jax.ShapeDtypeStruct((groups, wide), jnp.float32),
        ],
        scratch_shapes=[
            pltpu.VMEM((groups, held, wide), jnp.bfloat16),
            pltpu.VMEM((groups, wide, units), jnp.bfloat16),
            pltpu.VMEM((groups, wide, units), jnp.bfloat16),
            pltpu.VMEM((rows, units), jnp.float32),
            pltpu.VMEM((rows, units), jnp.float32),
            pltpu.VMEM((rows, 1), jnp.float32),
            pltpu.SemaphoreType.DMA((n,)),
            pltpu.SemaphoreType.DMA((n,)),
            pltpu.SemaphoreType.DMA((n,)),
        ],
        compiler_params=pltpu.CompilerParams(vmem_limit_bytes=30 * MIB),
        cost_estimate=HEAVY,
    )(owners, *pieces, in_hbm(w_gate), in_hbm(w_up), weight, gain.reshape(groups, wide))


def down_kernel(idx_ref, act_ref, w_ref, out_ref):
    m, _, width = out_ref.shape

    @pl.loop(0, m // 2)
    def _(j):
        even = idx_ref[2 * j] // 2 * 2
        swapped = idx_ref[2 * j] - even
        at = pl.ds(pl.multiple_of(even * width, 128), 2 * width)
        both = jnp.dot(act_ref[...], w_ref[:, at], preferred_element_type=jnp.float32)
        out_ref[2 * j + swapped] = both[:, :width].astype(jnp.bfloat16)
        out_ref[2 * j + 1 - swapped] = both[:, width:].astype(jnp.bfloat16)


def down(act, owners, w_down, width):
    rows, units = act.shape
    m = owners.shape[0]
    if width % 128 or m % 2:
        cut = [
            lax.dynamic_slice_in_dim(w_down, owners[j] * width, width, axis=1) for j in range(m)
        ]
        return jnp.stack(
            [jnp.dot(act, w, preferred_element_type=jnp.float32).astype(jnp.bfloat16) for w in cut]
        )
    return pl.pallas_call(
        down_kernel,
        in_specs=[SMEM, VMEM, VMEM],
        out_specs=VMEM,
        out_shape=jax.ShapeDtypeStruct((m, rows, width), jnp.bfloat16),
        compiler_params=pltpu.CompilerParams(vmem_limit_bytes=8 * MIB),
        cost_estimate=HEAVY,
    )(owners, act, w_down)


def combine_kernel(n, parts, near_ref, got_ref, *outs):
    size = near_ref.shape[1] // parts
    for p in range(parts):
        at = slice(p * size, (p + 1) * size)
        for d in range(n):
            both = near_ref[d, at, :].astype(jnp.float32) + got_ref[d, at, :].astype(jnp.float32)
            outs[p * n + d][...] = both.astype(outs[p * n + d].dtype)


def combine(near, got, parts):
    n, rows, width = near.shape
    outs = pl.pallas_call(
        functools.partial(combine_kernel, n, parts),
        in_specs=[VMEM] * 2,
        out_specs=[VMEM] * (n * parts),
        out_shape=[
            jax.ShapeDtypeStruct((rows // parts, width), jnp.bfloat16 if d else jnp.float32)
            for d in range(n)
        ]
        * parts,
        compiler_params=pltpu.CompilerParams(vmem_limit_bytes=12 * MIB),
        cost_estimate=HEAVY,
    )(near, got)
    return [outs[p * n : (p + 1) * n] for p in range(parts)]


def reduce_kernel(n, blocks, *refs):
    pieces, outs = refs[:n], refs[-blocks:]
    size = outs[0].shape[0]
    for b in range(blocks):
        at = slice(b * size, (b + 1) * size)
        total = pieces[0][at, :]
        for piece in pieces[1:]:
            total = total + piece[at, :].astype(jnp.float32)
        outs[b][...] = total.astype(outs[b].dtype)


def reduce(pieces, blocks, own, after):
    n = len(pieces)
    rows, width = pieces[0].shape
    return pl.pallas_call(
        functools.partial(reduce_kernel, n, blocks),
        in_specs=[VMEM] * n + [ANY] * len(after),
        out_specs=[VMEM] * blocks,
        out_shape=[
            jax.ShapeDtypeStruct((rows // blocks, width), jnp.bfloat16 if b or not own else jnp.float32)
            for b in range(blocks)
        ],
        compiler_params=pltpu.CompilerParams(vmem_limit_bytes=8 * MIB),
        cost_estimate=HEAVY,
    )(*pieces, *after)


def finish_kernel(counts, per, *refs):
    out_ref = refs[-1]
    chunks = len(counts)
    part = out_ref.shape[0] // (chunks * per)
    for c in range(chunks):
        pieces = refs[sum(counts[:c]) : sum(counts[: c + 1])]
        for p in range(per):
            at = slice(p * part, (p + 1) * part)
            total = pieces[0][at, :]
            for piece in pieces[1:]:
                total = total + piece[at, :].astype(jnp.float32)
            start = (p * chunks + c) * part
            out_ref[start : start + part, :] = total.astype(jnp.bfloat16)


def finish(terms, per):
    counts = [len(chunk) for chunk in terms]
    rows, width = terms[0][0].shape
    return pl.pallas_call(
        functools.partial(finish_kernel, counts, per),
        in_specs=[VMEM] * sum(counts),
        out_specs=VMEM,
        out_shape=jax.ShapeDtypeStruct((len(counts) * rows, width), jnp.bfloat16),
        compiler_params=pltpu.CompilerParams(vmem_limit_bytes=8 * MIB),
        cost_estimate=HEAVY,
    )(*[x for chunk in terms for x in chunk])


def attend_kernel(scale, chunk, len_ref, q_ref, c_ref, w_hbm, *refs):
    out_ref, w_ref, score_ref, prob_ref, lat_ref, sem = refs[-6:]
    step, steps = pl.program_id(0), pl.num_programs(0)
    group, heads, _ = q_ref.shape
    slots = c_ref.shape[2]
    _, latent_width, size = w_ref.shape
    load = pltpu.make_async_copy(w_hbm, w_ref, sem)

    @pl.when(step == 0)
    def _():
        load.start()

    places = lax.broadcasted_iota(jnp.int32, (heads, slots), 1)
    for r in range(group):
        scores = jnp.dot(q_ref[r], c_ref[r], preferred_element_type=jnp.float32) * scale
        live = len_ref[(chunk * steps + step) * group + r]
        score_ref[r * heads : (r + 1) * heads, :] = jnp.where(places < live, scores, -jnp.inf)
    scores = score_ref[...]
    exp_terms = jnp.exp(scores - jnp.max(scores, axis=1, keepdims=True))
    probs = exp_terms / jnp.sum(exp_terms, axis=1, keepdims=True)
    prob_ref[...] = probs.astype(jnp.bfloat16)
    for r in range(group):
        latent = lax.dot_general(
            prob_ref[r * heads : (r + 1) * heads, :],
            c_ref[r, :latent_width, :],
            (((1,), (1,)), ((), ())),
            preferred_element_type=jnp.float32,
        )
        at = pl.ds(pl.multiple_of((step * group + r) * heads, heads), heads)
        for k in range(latent_width // 128):
            lat_ref[k, at, :] = latent[:, k * 128 : (k + 1) * 128]

    @pl.when(step == steps - 1)
    def _():
        load.wait()
        for h in range(heads):
            at = pl.ds(h, out_ref.shape[0], stride=heads)
            latent = jnp.concatenate(
                [lat_ref[k, at, :] for k in range(latent_width // 128)], axis=1
            ).astype(jnp.bfloat16)
            out_ref[:, h * size : (h + 1) * size] = jnp.dot(
                latent, w_ref[h], preferred_element_type=jnp.float32
            ).astype(jnp.bfloat16)


def attend(queries, cache, lengths, w_uv, chunk, chunks, after):
    rows, heads, entries = queries.shape
    slots = cache.shape[1]
    _, latent_width, size = w_uv.shape
    group = 16
    steps = rows // chunks // group
    return pl.pallas_call(
        functools.partial(attend_kernel, (size + ROPE) ** (-0.5), chunk),
        grid_spec=pltpu.PrefetchScalarGridSpec(
            num_scalar_prefetch=1,
            grid=(steps,),
            in_specs=[
                pl.BlockSpec((group, heads, entries), lambda i, _: (chunk * steps + i, 0, 0)),
                pl.BlockSpec((group, entries, slots), lambda i, _: (chunk * steps + i, 0, 0)),
                ANY,
            ]
            + [ANY] * len(after),
            out_specs=pl.BlockSpec((steps * group, heads * size), lambda i, _: (0, 0)),
            scratch_shapes=[
                pltpu.VMEM(w_uv.shape, jnp.bfloat16),
                pltpu.VMEM((group * heads, slots), jnp.float32),
                pltpu.VMEM((group * heads, slots), jnp.bfloat16),
                pltpu.VMEM((latent_width // 128, steps * group * heads, 128), jnp.float32),
                pltpu.SemaphoreType.DMA,
            ],
        ),
        out_shape=jax.ShapeDtypeStruct((steps * group, heads * size), jnp.bfloat16),
        compiler_params=pltpu.CompilerParams(vmem_limit_bytes=20 * MIB),
        cost_estimate=HEAVY,
    )(
        lengths,
        in_hbm(queries),
        in_hbm(jnp.swapaxes(cache, 1, 2)),
        in_hbm(w_uv),
        *after,
    )


def shards(
    n_row,
    n_col,
    queries,
    cache,
    lengths,
    w_uv,
    w_out,
    residual_in,
    norm_gain,
    expert_ids,
    gate_vals,
    w_gate,
    w_up,
    w_down,
):
    side, row, col = lax.axis_index("side"), lax.axis_index("row"), lax.axis_index("col")
    block, width = residual_in.shape
    height = queries.shape[0]
    per = block // height
    chunks = 2
    part = height // chunks
    owners = jnp.stack(
        [(side ^ ds) * n_row + (row ^ d) for ds in range(2) for d in range(n_row)]
    ).astype(jnp.int32)
    places = (((owners // per) ^ col) * per + owners % per).astype(jnp.int32)

    chosen = expert_ids == owners[0]
    my_gate = jnp.sum(jnp.where(chosen, gate_vals, 0.0), axis=1)[None, :]
    gain = jnp.broadcast_to(norm_gain, (EXTRA, width))

    first = attend(queries, cache, lengths, w_uv, 0, chunks, [])
    second = attend(queries, cache, lengths, w_uv, 1, chunks, [first])
    gate_dev, up_dev, down_dev = w_gate[0], w_up[0], w_down[0]

    def over_col(pieces):
        return [pieces[0]] + [swap(pieces[d], "col", n_col, d) for d in range(1, n_col)]

    def over_row(pieces):
        return [pieces[0]] + [swap(pieces[d], "row", n_row, d) for d in range(1, n_row)]

    def other_core(x):
        return swap(x, "side", 2, 1)

    def experts(near, held, inverse_gain, parts):
        far = [other_core(piece) for piece in near]
        act, inverse_gain = gate_up(
            near + far, owners, gate_dev, up_dev, held, inverse_gain
        )
        far_rows = down(act, owners[n_row:], down_dev, width)
        near_rows = down(act, owners[:n_row], down_dev, width)
        return combine(near_rows, other_core(far_rows), parts), inverse_gain

    def stack_rows(x, after, estimate=HEAVY):
        return stack(over_row([x] * n_row), after, estimate).reshape(n_row, *x.shape)

    near_0 = stack_rows(first, [second], STACK)
    partial_0 = project(near_0, other_core(near_0), places, w_out, n_col, [], [])
    near_1 = stack_rows(second, partial_0[:1], STACK)
    hidden_0, scaled_0 = norm(residual_in, norm_gain, over_col(partial_0), 0, per, 0, [])
    partial_1 = project(near_1, other_core(near_1), places, w_out, n_col, [my_gate], [scaled_0])
    rows_0 = stack(over_col([scaled_0] * n_col) + [gain], partial_1[:1])
    hidden_1, scaled_1, gates = norm(
        residual_in, norm_gain, over_col(partial_1), 1, per, 1, [rows_0]
    )
    weight = gates.reshape(n_col, per, chunks, part)
    weight = [weight[:, :, c].reshape(-1, 1) for c in range(chunks)]
    near_0 = over_row([rows_0] * n_row)
    no_gain = jnp.zeros((2 * n_row, width), jnp.float32)
    [both_0], inverse_gain = experts(near_0, weight[0], no_gain, 1)
    rows_1 = stack(over_col([scaled_1] * n_col), near_0[1:])
    near_1 = stack_rows(rows_1, both_0[:1])
    both_1, _ = experts([near_1], hand_on(weight[1], [near_1]), inverse_gain, 2)
    total_0 = reduce(over_row(both_0), n_col, True, both_1[0][:1])
    terms_0 = [hidden_0, *over_col(total_0)]
    half = n_col // 2
    far_1 = reduce(over_row(both_1[1]), half, False, total_0[:1])
    last = [swap(far_1[d], "col", n_col, half + d) for d in range(half)]
    total_1 = reduce(over_row(both_1[0]), half, True, [far_1[0], *terms_0[2:]])
    first = [total_1[0]] + [swap(total_1[d], "col", n_col, d) for d in range(1, half)]
    [hidden_1] = reduce([hidden_1, *last], 1, True, total_1[:1])
    return finish([terms_0, [hidden_1, *first]], per)


def solution(mesh):
    placed = (
        P(("side", "row"), "col", None),
        P(("side", "row"), None, None),
        P(("side", "row")),
        P("col", None, None),
        P("col", ("side", "row")),
        P("col", ("side", "row")),
        P(("side", "row")),
        P("col", None),
        P("col", None),
        P(("side", "row"), None, "col"),
        P(("side", "row"), None, "col"),
        P(("side", "row"), "col", None),
    )
    return jax.shard_map(
        functools.partial(shards, mesh.shape["row"], mesh.shape["col"]),
        mesh=mesh,
        in_specs=placed,
        out_specs=P("col", ("side", "row")),
        check_vma=False,
    )
```

```python
import functools

import jax
import jax.numpy as jnp
from jax import lax
from jax.experimental import pallas as pl
from jax.experimental.pallas import tpu as pltpu
from jax.sharding import PartitionSpec as P

ROPE = 64
EPS = 1e-06
MIB = 1024 * 1024
EXTRA = 16
ANY = pl.BlockSpec(memory_space=pl.ANY)
VMEM = pl.BlockSpec(memory_space=pltpu.VMEM)
SMEM = pl.BlockSpec(memory_space=pltpu.SMEM)


def cost(us):
    return pl.CostEstimate(flops=int(us * 1e9), bytes_accessed=1024, transcendentals=0)


LIGHT, STACK, HEAVY = cost(0.001), cost(0.5), cost(100)


def in_hbm(x):
    return pltpu.with_memory_space_constraint(x, pltpu.HBM)


def swap(x, axis, count, d):
    return lax.ppermute(x, axis, [(i, i ^ d) for i in range(count)])


def stack_kernel(n, *refs):
    pieces, (out_ref, held_ref, in_sems, out_sems) = refs[:n], refs[-4:]
    loads, stores, start = [], [], 0
    for i in range(n):
        height = pieces[i].shape[0]
        at = held_ref.at[pl.ds(start, height)]
        loads.append(pltpu.make_async_copy(pieces[i], at, in_sems.at[i]))
        stores.append(
            pltpu.make_async_copy(at, out_ref.at[pl.ds(start, height)], out_sems.at[i])
        )
        start += height
    for load in loads:
        load.start()
    for load, store in zip(loads, stores):
        load.wait()
        store.start()
    for store in stores:
        store.wait()


def stack(pieces, after, estimate=HEAVY):
    n = len(pieces)
    shape = (sum(piece.shape[0] for piece in pieces), pieces[0].shape[1])
    return pl.pallas_call(
        functools.partial(stack_kernel, n),
        in_specs=[ANY] * (n + len(after)),
        out_specs=ANY,
        out_shape=jax.ShapeDtypeStruct(shape, pieces[0].dtype),
        scratch_shapes=[
            pltpu.VMEM(shape, pieces[0].dtype),
            pltpu.SemaphoreType.DMA((n,)),
            pltpu.SemaphoreType.DMA((n,)),
        ],
        compiler_params=pltpu.CompilerParams(vmem_limit_bytes=8 * MIB),
        cost_estimate=estimate,
    )(*pieces, *after)


def hand_on_kernel(x_ref, *refs):
    refs[-1][...] = x_ref[...]


def hand_on(x, after):
    return pl.pallas_call(
        hand_on_kernel,
        in_specs=[VMEM] + [ANY] * len(after),
        out_specs=VMEM,
        out_shape=jax.ShapeDtypeStruct(x.shape, x.dtype),
        compiler_params=pltpu.CompilerParams(vmem_limit_bytes=2 * MIB),
        cost_estimate=HEAVY,
    )(x, *after)


def project_kernel(blocks, n_gate, pos_ref, near_ref, far_ref, w_hbm, *refs):
    outs, (rows_ref, w_ref, acc_ref, sems, w_sems) = refs[-5 - blocks : -5], refs[-5:]
    half, height, full = near_ref.shape
    n = 2 * half
    pieces = [near_ref.at[i] for i in range(half)] + [far_ref.at[i] for i in range(half)]
    copies = [
        pltpu.make_async_copy(
            pieces[i],
            rows_ref.at[pl.ds(pl.multiple_of(pos_ref[i] * height, height), height)],
            sems.at[i],
        )
        for i in range(n)
    ]
    depth = min(512, full)

    def load(k):
        at = pl.ds(pl.multiple_of(k * depth, depth), depth)
        return pltpu.make_async_copy(w_hbm.at[at], w_ref.at[at], w_sems.at[k])

    for copy in copies:
        copy.start()
    for k in range(full // depth):
        load(k).start()
    acc_ref[...] = jnp.zeros_like(acc_ref)
    for copy in copies:
        copy.wait()

    @pl.loop(0, full // depth)
    def _(k):
        load(k).wait()
        at = pl.ds(pl.multiple_of(k * depth, depth), depth)
        acc_ref[...] += jnp.dot(
            rows_ref[:, at], w_ref[at, :], preferred_element_type=jnp.float32
        )

    size = acc_ref.shape[0] // blocks
    for d in range(blocks):
        outs[d][:size, :] = acc_ref[d * size : (d + 1) * size, :].astype(jnp.bfloat16)
    if n_gate:
        gate_ref = refs[0]
        rest, parts = gate_ref[...], []
        for _ in range(3):
            parts.append(rest.astype(jnp.bfloat16).astype(jnp.float32))
            rest = rest - parts[-1]
        parts.append(jnp.zeros((EXTRA - 3, rest.shape[1]), jnp.float32))
        parts = jnp.concatenate(parts, axis=0).astype(jnp.bfloat16)
        for d in range(blocks):
            outs[d][size:, :] = jnp.zeros((EXTRA, outs[d].shape[1]), jnp.bfloat16)
            outs[d][size:, : rest.shape[1]] = parts


def project(near, far, places, w_out, blocks, gate, after):
    half, height, full = near.shape
    n = 2 * half
    width = w_out.shape[1]
    rows = n * height
    held = rows // blocks + EXTRA * len(gate)
    return pl.pallas_call(
        functools.partial(project_kernel, blocks, len(gate)),
        in_specs=[SMEM, ANY, ANY, ANY] + [VMEM] * len(gate) + [ANY] * len(after),
        out_specs=[VMEM] * blocks,
        out_shape=[jax.ShapeDtypeStruct((held, width), jnp.bfloat16)] * blocks,
        scratch_shapes=[
            pltpu.VMEM((rows, full), jnp.bfloat16),
            pltpu.VMEM(w_out.shape, jnp.bfloat16),
            pltpu.VMEM((rows, width), jnp.float32),
            pltpu.SemaphoreType.DMA((n,)),
            pltpu.SemaphoreType.DMA((full // min(512, full),)),
        ],
        compiler_params=pltpu.CompilerParams(vmem_limit_bytes=18 * MIB),
        cost_estimate=HEAVY,
    )(places, near, far, in_hbm(w_out), *gate, *after)


def norm_kernel(chunk, per, n, n_gate, residual_ref, gain_ref, *refs):
    pieces, outs = refs[:n], refs[len(refs) - 2 - n_gate :]
    hidden_ref, scaled_ref = outs[:2]
    rows = hidden_ref.shape[0]
    part = rows // per
    height = residual_ref.shape[0] // per
    for p in range(per):
        to = slice(p * part, (p + 1) * part)
        start = p * height + chunk * part
        hidden = residual_ref[start : start + part, :].astype(jnp.float32)
        for piece in pieces:
            hidden = hidden + piece[to, :].astype(jnp.float32)
        hidden_ref[to, :] = hidden
        scaled_ref[to, :] = (hidden * gain_ref[...].astype(jnp.float32)).astype(jnp.bfloat16)
    if n_gate:
        for d in range(n):
            parts = pieces[d][rows:, : outs[2].shape[1]].astype(jnp.float32)
            outs[2][d : d + 1, :] = parts[0:1] + parts[1:2] + parts[2:3]


def norm(residual, gain, pieces, chunk, per, n_gate, after):
    n = len(pieces)
    block, width = residual.shape
    shape = (pieces[0].shape[0] - EXTRA * n_gate, width)
    return pl.pallas_call(
        functools.partial(norm_kernel, chunk, per, n, n_gate),
        in_specs=[VMEM] * (n + 2) + [ANY] * len(after),
        out_specs=[VMEM] * (2 + n_gate),
        out_shape=[
            jax.ShapeDtypeStruct(shape, jnp.float32),
            jax.ShapeDtypeStruct(shape, jnp.bfloat16),
        ]
        + [jax.ShapeDtypeStruct((n, block), jnp.float32)] * n_gate,
        compiler_params=pltpu.CompilerParams(vmem_limit_bytes=4 * MIB),
        cost_estimate=HEAVY,
    )(residual, gain[None, :], *pieces, *after)


def gate_up_kernel(n_ref, idx_ref, *refs):
    pieces = []
    for ref in refs[:n_ref]:
        pieces += [ref] if len(ref.shape) == 2 else [ref.at[i] for i in range(ref.shape[0])]
    n = len(pieces)
    wg_hbm, wu_hbm, weight_ref, gain_in = refs[n_ref : n_ref + 4]
    out_ref, gain_ref, x_ref, wg_ref, wu_ref, g_ref, u_ref, sq_ref, sems, wg_sems, wu_sems = refs[-11:]
    width = pieces[0].shape[1]
    rows = out_ref.shape[0]
    group = n // x_ref.shape[0]

    def load(i, j):
        at = pl.ds(pl.multiple_of(idx_ref[i * group + j] * width, width), width)
        to = pl.ds(j * width, width)
        return (
            pltpu.make_async_copy(pieces[0], x_ref.at[i, :, to], sems.at[i * group + j]),
            pltpu.make_async_copy(wg_hbm.at[at], wg_ref.at[i, to], wg_sems.at[i * group + j]),
            pltpu.make_async_copy(wu_hbm.at[at], wu_ref.at[i, to], wu_sems.at[i * group + j]),
        )

    for i in range(n):
        to = x_ref.at[i // group, :, pl.ds(i % group * width, width)]
        pltpu.make_async_copy(pieces[i], to, sems.at[i]).start()
        for copy in load(i // group, i % group)[1:]:
            copy.start()
    g_ref[...] = jnp.zeros_like(g_ref)
    u_ref[...] = jnp.zeros_like(u_ref)
    sq_ref[...] = jnp.zeros_like(sq_ref)
    gain_ref[...] = gain_in[...]

    @pl.loop(0, n // group)
    def _(i):
        for j in range(group):
            for copy in load(i, j):
                copy.wait()
        x = x_ref[i, :rows, :]
        if x_ref.shape[1] > rows:
            gain_ref[pl.ds(i, 1), :] = 1.0 / x_ref[i, rows:, :][0:1].astype(jnp.float32)
        g_ref[...] += jnp.dot(x, wg_ref[i], preferred_element_type=jnp.float32)
        u_ref[...] += jnp.dot(x, wu_ref[i], preferred_element_type=jnp.float32)
        hidden = x.astype(jnp.float32) * gain_ref[pl.ds(i, 1), :]
        sq_ref[...] += jnp.sum(hidden * hidden, axis=1, keepdims=True)

    inv = lax.rsqrt(sq_ref[...] / (n * width) + EPS)
    g = g_ref[...] * inv
    u = u_ref[...] * inv
    out_ref[...] = (g / (1.0 + jnp.exp(-g)) * u * weight_ref[...]).astype(jnp.bfloat16)


def gate_up(pieces, owners, w_gate, w_up, weight, gain):
    n = owners.shape[0]
    held, width = pieces[0].shape[-2:]
    rows = weight.shape[0]
    full, units = w_gate.shape
    group = 2 if width % 128 == 0 else 1
    groups, wide = n // group, group * width
    return pl.pallas_call(
        functools.partial(gate_up_kernel, len(pieces)),
        in_specs=[SMEM] + [ANY] * (len(pieces) + 2) + [VMEM] * 2,
        out_specs=[VMEM] * 2,
        out_shape=[
            jax.ShapeDtypeStruct((rows, units), jnp.bfloat16),
            jax.ShapeDtypeStruct((groups, wide), jnp.float32),
        ],
        scratch_shapes=[
            pltpu.VMEM((groups, held, wide), jnp.bfloat16),
            pltpu.VMEM((groups, wide, units), jnp.bfloat16),
            pltpu.VMEM((groups, wide, units), jnp.bfloat16),
            pltpu.VMEM((rows, units), jnp.float32),
            pltpu.VMEM((rows, units), jnp.float32),
            pltpu.VMEM((rows, 1), jnp.float32),
            pltpu.SemaphoreType.DMA((n,)),
            pltpu.SemaphoreType.DMA((n,)),
            pltpu.SemaphoreType.DMA((n,)),
        ],
        compiler_params=pltpu.CompilerParams(vmem_limit_bytes=30 * MIB),
        cost_estimate=HEAVY,
    )(owners, *pieces, in_hbm(w_gate), in_hbm(w_up), weight, gain.reshape(groups, wide))


def down_kernel(idx_ref, act_ref, w_ref, out_ref):
    m, _, width = out_ref.shape

    @pl.loop(0, m // 2)
    def _(j):
        even = idx_ref[2 * j] // 2 * 2
        swapped = idx_ref[2 * j] - even
        at = pl.ds(pl.multiple_of(even * width, 128), 2 * width)
        both = jnp.dot(act_ref[...], w_ref[:, at], preferred_element_type=jnp.float32)
        out_ref[2 * j + swapped] = both[:, :width].astype(jnp.bfloat16)
        out_ref[2 * j + 1 - swapped] = both[:, width:].astype(jnp.bfloat16)


def down(act, owners, w_down, width):
    rows, units = act.shape
    m = owners.shape[0]
    if width % 128 or m % 2:
        cut = [
            lax.dynamic_slice_in_dim(w_down, owners[j] * width, width, axis=1) for j in range(m)
        ]
        return jnp.stack(
            [jnp.dot(act, w, preferred_element_type=jnp.float32).astype(jnp.bfloat16) for w in cut]
        )
    return pl.pallas_call(
        down_kernel,
        in_specs=[SMEM, VMEM, VMEM],
        out_specs=VMEM,
        out_shape=jax.ShapeDtypeStruct((m, rows, width), jnp.bfloat16),
        compiler_params=pltpu.CompilerParams(vmem_limit_bytes=8 * MIB),
        cost_estimate=HEAVY,
    )(owners, act, w_down)


def combine_kernel(n, parts, near_ref, got_ref, *outs):
    size = near_ref.shape[1] // parts
    for p in range(parts):
        at = slice(p * size, (p + 1) * size)
        for d in range(n):
            both = near_ref[d, at, :].astype(jnp.float32) + got_ref[d, at, :].astype(jnp.float32)
            outs[p * n + d][...] = both.astype(outs[p * n + d].dtype)


def combine(near, got, parts):
    n, rows, width = near.shape
    outs = pl.pallas_call(
        functools.partial(combine_kernel, n, parts),
        in_specs=[VMEM] * 2,
        out_specs=[VMEM] * (n * parts),
        out_shape=[
            jax.ShapeDtypeStruct((rows // parts, width), jnp.bfloat16 if d else jnp.float32)
            for d in range(n)
        ]
        * parts,
        compiler_params=pltpu.CompilerParams(vmem_limit_bytes=12 * MIB),
        cost_estimate=HEAVY,
    )(near, got)
    return [outs[p * n : (p + 1) * n] for p in range(parts)]


def reduce_kernel(n, blocks, *refs):
    pieces, outs = refs[:n], refs[-blocks:]
    size = outs[0].shape[0]
    for b in range(blocks):
        at = slice(b * size, (b + 1) * size)
        total = pieces[0][at, :]
        for piece in pieces[1:]:
            total = total + piece[at, :].astype(jnp.float32)
        outs[b][...] = total.astype(outs[b].dtype)


def reduce(pieces, blocks, own, after):
    n = len(pieces)
    rows, width = pieces[0].shape
    return pl.pallas_call(
        functools.partial(reduce_kernel, n, blocks),
        in_specs=[VMEM] * n + [ANY] * len(after),
        out_specs=[VMEM] * blocks,
        out_shape=[
            jax.ShapeDtypeStruct((rows // blocks, width), jnp.bfloat16 if b or not own else jnp.float32)
            for b in range(blocks)
        ],
        compiler_params=pltpu.CompilerParams(vmem_limit_bytes=8 * MIB),
        cost_estimate=HEAVY,
    )(*pieces, *after)


def finish_kernel(counts, per, *refs):
    out_ref = refs[-1]
    chunks = len(counts)
    part = out_ref.shape[0] // (chunks * per)
    for c in range(chunks):
        pieces = refs[sum(counts[:c]) : sum(counts[: c + 1])]
        for p in range(per):
            at = slice(p * part, (p + 1) * part)
            total = pieces[0][at, :]
            for piece in pieces[1:]:
                total = total + piece[at, :].astype(jnp.float32)
            start = (p * chunks + c) * part
            out_ref[start : start + part, :] = total.astype(jnp.bfloat16)


def finish(terms, per):
    counts = [len(chunk) for chunk in terms]
    rows, width = terms[0][0].shape
    return pl.pallas_call(
        functools.partial(finish_kernel, counts, per),
        in_specs=[VMEM] * sum(counts),
        out_specs=VMEM,
        out_shape=jax.ShapeDtypeStruct((len(counts) * rows, width), jnp.bfloat16),
        compiler_params=pltpu.CompilerParams(vmem_limit_bytes=8 * MIB),
        cost_estimate=HEAVY,
    )(*[x for chunk in terms for x in chunk])


def attend_kernel(scale, chunk, len_ref, q_ref, c_ref, w_hbm, *refs):
    out_ref, w_ref, score_ref, prob_ref, lat_ref, sem = refs[-6:]
    step, steps = pl.program_id(0), pl.num_programs(0)
    group, heads, _ = q_ref.shape
    slots = c_ref.shape[2]
    _, latent_width, size = w_ref.shape
    load = pltpu.make_async_copy(w_hbm, w_ref, sem)

    @pl.when(step == 0)
    def _():
        load.start()

    places = lax.broadcasted_iota(jnp.int32, (heads, slots), 1)
    for r in range(group):
        scores = jnp.dot(q_ref[r], c_ref[r], preferred_element_type=jnp.float32) * scale
        live = len_ref[(chunk * steps + step) * group + r]
        score_ref[r * heads : (r + 1) * heads, :] = jnp.where(places < live, scores, -jnp.inf)
    scores = score_ref[...]
    exp_terms = jnp.exp(scores - jnp.max(scores, axis=1, keepdims=True))
    probs = exp_terms / jnp.sum(exp_terms, axis=1, keepdims=True)
    prob_ref[...] = probs.astype(jnp.bfloat16)
    for r in range(group):
        latent = lax.dot_general(
            prob_ref[r * heads : (r + 1) * heads, :],
            c_ref[r, :latent_width, :],
            (((1,), (1,)), ((), ())),
            preferred_element_type=jnp.float32,
        )
        at = pl.ds(pl.multiple_of((step * group + r) * heads, heads), heads)
        for k in range(latent_width // 128):
            lat_ref[k, at, :] = latent[:, k * 128 : (k + 1) * 128]

    @pl.when(step == steps - 1)
    def _():
        load.wait()
        for h in range(heads):
            at = pl.ds(h, out_ref.shape[0], stride=heads)
            latent = jnp.concatenate(
                [lat_ref[k, at, :] for k in range(latent_width // 128)], axis=1
            ).astype(jnp.bfloat16)
            out_ref[:, h * size : (h + 1) * size] = jnp.dot(
                latent, w_ref[h], preferred_element_type=jnp.float32
            ).astype(jnp.bfloat16)


def attend(queries, cache, lengths, w_uv, chunk, chunks, after):
    rows, heads, entries = queries.shape
    slots = cache.shape[1]
    _, latent_width, size = w_uv.shape
    group = 16
    steps = rows // chunks // group
    return pl.pallas_call(
        functools.partial(attend_kernel, (size + ROPE) ** (-0.5), chunk),
        grid_spec=pltpu.PrefetchScalarGridSpec(
            num_scalar_prefetch=1,
            grid=(steps,),
            in_specs=[
                pl.BlockSpec((group, heads, entries), lambda i, _: (chunk * steps + i, 0, 0)),
                pl.BlockSpec((group, entries, slots), lambda i, _: (chunk * steps + i, 0, 0)),
                ANY,
            ]
            + [ANY] * len(after),
            out_specs=pl.BlockSpec((steps * group, heads * size), lambda i, _: (0, 0)),
            scratch_shapes=[
                pltpu.VMEM(w_uv.shape, jnp.bfloat16),
                pltpu.VMEM((group * heads, slots), jnp.float32),
                pltpu.VMEM((group * heads, slots), jnp.bfloat16),
                pltpu.VMEM((latent_width // 128, steps * group * heads, 128), jnp.float32),
                pltpu.SemaphoreType.DMA,
            ],
        ),
        out_shape=jax.ShapeDtypeStruct((steps * group, heads * size), jnp.bfloat16),
        compiler_params=pltpu.CompilerParams(vmem_limit_bytes=20 * MIB),
        cost_estimate=HEAVY,
    )(
        lengths,
        in_hbm(queries),
        in_hbm(jnp.swapaxes(cache, 1, 2)),
        in_hbm(w_uv),
        *after,
    )


def shards(
    n_row,
    n_col,
    queries,
    cache,
    lengths,
    w_uv,
    w_out,
    residual_in,
    norm_gain,
    expert_ids,
    gate_vals,
    w_gate,
    w_up,
    w_down,
):
    side, row, col = lax.axis_index("side"), lax.axis_index("row"), lax.axis_index("col")
    block, width = residual_in.shape
    height = queries.shape[0]
    per = block // height
    chunks = 2
    part = height // chunks
    owners = jnp.stack(
        [(side ^ ds) * n_row + (row ^ d) for ds in range(2) for d in range(n_row)]
    ).astype(jnp.int32)
    places = (((owners // per) ^ col) * per + owners % per).astype(jnp.int32)

    chosen = expert_ids == owners[0]
    my_gate = jnp.sum(jnp.where(chosen, gate_vals, 0.0), axis=1)[None, :]
    gain = jnp.broadcast_to(norm_gain, (EXTRA, width))

    first = attend(queries, cache, lengths, w_uv, 0, chunks, [])
    second = attend(queries, cache, lengths, w_uv, 1, chunks, [first])
    gate_dev, up_dev, down_dev = w_gate[0], w_up[0], w_down[0]

    def over_col(pieces):
        return [pieces[0]] + [swap(pieces[d], "col", n_col, d) for d in range(1, n_col)]

    def over_row(pieces):
        return [pieces[0]] + [swap(pieces[d], "row", n_row, d) for d in range(1, n_row)]

    def other_core(x):
        return swap(x, "side", 2, 1)

    def experts(near, held, inverse_gain, parts):
        far = [other_core(piece) for piece in near]
        act, inverse_gain = gate_up(
            near + far, owners, gate_dev, up_dev, held, inverse_gain
        )
        far_rows = down(act, owners[n_row:], down_dev, width)
        near_rows = down(act, owners[:n_row], down_dev, width)
        return combine(near_rows, other_core(far_rows), parts), inverse_gain

    def stack_rows(x, after, estimate=HEAVY):
        return stack(over_row([x] * n_row), after, estimate).reshape(n_row, *x.shape)

    near_0 = stack_rows(first, [second], STACK)
    partial_0 = project(near_0, other_core(near_0), places, w_out, n_col, [], [])
    near_1 = stack_rows(second, partial_0[:1], STACK)
    hidden_0, scaled_0 = norm(residual_in, norm_gain, over_col(partial_0), 0, per, 0, [])
    partial_1 = project(near_1, other_core(near_1), places, w_out, n_col, [my_gate], [scaled_0])
    rows_0 = stack(over_col([scaled_0] * n_col) + [gain], partial_1[:1])
    hidden_1, scaled_1, gates = norm(
        residual_in, norm_gain, over_col(partial_1), 1, per, 1, [rows_0]
    )
    weight = gates.reshape(n_col, per, chunks, part)
    weight = [weight[:, :, c].reshape(-1, 1) for c in range(chunks)]
    near_0 = over_row([rows_0] * n_row)
    no_gain = jnp.zeros((2 * n_row, width), jnp.float32)
    [both_0], inverse_gain = experts(near_0, weight[0], no_gain, 1)
    rows_1 = stack(over_col([scaled_1] * n_col), near_0[1:])
    near_1 = stack_rows(rows_1, both_0[1:])
    both_1, _ = experts([near_1], hand_on(weight[1], [near_1]), inverse_gain, 2)
    total_0 = reduce(over_row(both_0), n_col, True, both_1[0][:1])
    terms_0 = [hidden_0, *over_col(total_0)]
    half = n_col // 2
    far_1 = reduce(over_row(both_1[1]), half, False, total_0[:1])
    last = [swap(far_1[d], "col", n_col, half + d) for d in range(half)]
    total_1 = reduce(over_row(both_1[0]), half, True, [far_1[0], *terms_0[2:]])
    first = [total_1[0]] + [swap(total_1[d], "col", n_col, d) for d in range(1, half)]
    [hidden_1] = reduce([hidden_1, *last], 1, True, total_1[:1])
    return finish([terms_0, [hidden_1, *first]], per)


def solution(mesh):
    placed = (
        P(("side", "row"), "col", None),
        P(("side", "row"), None, None),
        P(("side", "row")),
        P("col", None, None),
        P("col", ("side", "row")),
        P("col", ("side", "row")),
        P(("side", "row")),
        P("col", None),
        P("col", None),
        P(("side", "row"), None, "col"),
        P(("side", "row"), None, "col"),
        P(("side", "row"), "col", None),
    )
    return jax.shard_map(
        functools.partial(shards, mesh.shape["row"], mesh.shape["col"]),
        mesh=mesh,
        in_specs=placed,
        out_specs=P("col", ("side", "row")),
        check_vma=False,
    )
```

```python
import functools

import jax
import jax.numpy as jnp
from jax import lax
from jax.experimental import pallas as pl
from jax.experimental.pallas import tpu as pltpu
from jax.sharding import PartitionSpec as P

ROPE = 64
EPS = 1e-06
MIB = 1024 * 1024
EXTRA = 16
ANY = pl.BlockSpec(memory_space=pl.ANY)
VMEM = pl.BlockSpec(memory_space=pltpu.VMEM)
SMEM = pl.BlockSpec(memory_space=pltpu.SMEM)


def cost(us):
    return pl.CostEstimate(flops=int(us * 1e9), bytes_accessed=1024, transcendentals=0)


LIGHT, STACK, HEAVY = cost(0.001), cost(0.5), cost(100)


def in_hbm(x):
    return pltpu.with_memory_space_constraint(x, pltpu.HBM)


def swap(x, axis, count, d):
    return lax.ppermute(x, axis, [(i, i ^ d) for i in range(count)])


def stack_kernel(n, *refs):
    pieces, (out_ref, held_ref, in_sems, out_sems) = refs[:n], refs[-4:]
    loads, stores, start = [], [], 0
    for i in range(n):
        height = pieces[i].shape[0]
        at = held_ref.at[pl.ds(start, height)]
        loads.append(pltpu.make_async_copy(pieces[i], at, in_sems.at[i]))
        stores.append(
            pltpu.make_async_copy(at, out_ref.at[pl.ds(start, height)], out_sems.at[i])
        )
        start += height
    for load in loads:
        load.start()
    for load, store in zip(loads, stores):
        load.wait()
        store.start()
    for store in stores:
        store.wait()


def stack(pieces, after, estimate=HEAVY):
    n = len(pieces)
    shape = (sum(piece.shape[0] for piece in pieces), pieces[0].shape[1])
    return pl.pallas_call(
        functools.partial(stack_kernel, n),
        in_specs=[ANY] * (n + len(after)),
        out_specs=ANY,
        out_shape=jax.ShapeDtypeStruct(shape, pieces[0].dtype),
        scratch_shapes=[
            pltpu.VMEM(shape, pieces[0].dtype),
            pltpu.SemaphoreType.DMA((n,)),
            pltpu.SemaphoreType.DMA((n,)),
        ],
        compiler_params=pltpu.CompilerParams(vmem_limit_bytes=8 * MIB),
        cost_estimate=estimate,
    )(*pieces, *after)


def hand_on_kernel(x_ref, *refs):
    refs[-1][...] = x_ref[...]


def hand_on(x, after):
    return pl.pallas_call(
        hand_on_kernel,
        in_specs=[VMEM] + [ANY] * len(after),
        out_specs=VMEM,
        out_shape=jax.ShapeDtypeStruct(x.shape, x.dtype),
        compiler_params=pltpu.CompilerParams(vmem_limit_bytes=2 * MIB),
        cost_estimate=HEAVY,
    )(x, *after)


def project_kernel(blocks, n_gate, pos_ref, near_ref, far_ref, w_hbm, *refs):
    outs, (rows_ref, w_ref, acc_ref, sems, w_sems) = refs[-5 - blocks : -5], refs[-5:]
    half, height, full = near_ref.shape
    n = 2 * half
    pieces = [near_ref.at[i] for i in range(half)] + [far_ref.at[i] for i in range(half)]
    copies = [
        pltpu.make_async_copy(
            pieces[i],
            rows_ref.at[pl.ds(pl.multiple_of(pos_ref[i] * height, height), height)],
            sems.at[i],
        )
        for i in range(n)
    ]
    depth = min(512, full)

    def load(k):
        at = pl.ds(pl.multiple_of(k * depth, depth), depth)
        return pltpu.make_async_copy(w_hbm.at[at], w_ref.at[at], w_sems.at[k])

    for copy in copies:
        copy.start()
    for k in range(full // depth):
        load(k).start()
    acc_ref[...] = jnp.zeros_like(acc_ref)
    for copy in copies:
        copy.wait()

    @pl.loop(0, full // depth)
    def _(k):
        load(k).wait()
        at = pl.ds(pl.multiple_of(k * depth, depth), depth)
        acc_ref[...] += jnp.dot(
            rows_ref[:, at], w_ref[at, :], preferred_element_type=jnp.float32
        )

    size = acc_ref.shape[0] // blocks
    for d in range(blocks):
        outs[d][:size, :] = acc_ref[d * size : (d + 1) * size, :].astype(jnp.bfloat16)
    if n_gate:
        gate_ref = refs[0]
        rest, parts = gate_ref[...], []
        for _ in range(3):
            parts.append(rest.astype(jnp.bfloat16).astype(jnp.float32))
            rest = rest - parts[-1]
        parts.append(jnp.zeros((EXTRA - 3, rest.shape[1]), jnp.float32))
        parts = jnp.concatenate(parts, axis=0).astype(jnp.bfloat16)
        for d in range(blocks):
            outs[d][size:, :] = jnp.zeros((EXTRA, outs[d].shape[1]), jnp.bfloat16)
            outs[d][size:, : rest.shape[1]] = parts


def project(near, far, places, w_out, blocks, gate, after):
    half, height, full = near.shape
    n = 2 * half
    width = w_out.shape[1]
    rows = n * height
    held = rows // blocks + EXTRA * len(gate)
    return pl.pallas_call(
        functools.partial(project_kernel, blocks, len(gate)),
        in_specs=[SMEM, ANY, ANY, ANY] + [VMEM] * len(gate) + [ANY] * len(after),
        out_specs=[VMEM] * blocks,
        out_shape=[jax.ShapeDtypeStruct((held, width), jnp.bfloat16)] * blocks,
        scratch_shapes=[
            pltpu.VMEM((rows, full), jnp.bfloat16),
            pltpu.VMEM(w_out.shape, jnp.bfloat16),
            pltpu.VMEM((rows, width), jnp.float32),
            pltpu.SemaphoreType.DMA((n,)),
            pltpu.SemaphoreType.DMA((full // min(512, full),)),
        ],
        compiler_params=pltpu.CompilerParams(vmem_limit_bytes=18 * MIB),
        cost_estimate=HEAVY,
    )(places, near, far, in_hbm(w_out), *gate, *after)


def norm_kernel(chunk, per, n, n_gate, residual_ref, gain_ref, *refs):
    pieces, outs = refs[:n], refs[len(refs) - 2 - n_gate :]
    hidden_ref, scaled_ref = outs[:2]
    rows = hidden_ref.shape[0]
    part = rows // per
    height = residual_ref.shape[0] // per
    for p in range(per):
        to = slice(p * part, (p + 1) * part)
        start = p * height + chunk * part
        hidden = residual_ref[start : start + part, :].astype(jnp.float32)
        for piece in pieces:
            hidden = hidden + piece[to, :].astype(jnp.float32)
        hidden_ref[to, :] = hidden
        scaled_ref[to, :] = (hidden * gain_ref[...].astype(jnp.float32)).astype(jnp.bfloat16)
    if n_gate:
        for d in range(n):
            parts = pieces[d][rows:, : outs[2].shape[1]].astype(jnp.float32)
            outs[2][d : d + 1, :] = parts[0:1] + parts[1:2] + parts[2:3]


def norm(residual, gain, pieces, chunk, per, n_gate, after):
    n = len(pieces)
    block, width = residual.shape
    shape = (pieces[0].shape[0] - EXTRA * n_gate, width)
    return pl.pallas_call(
        functools.partial(norm_kernel, chunk, per, n, n_gate),
        in_specs=[VMEM] * (n + 2) + [ANY] * len(after),
        out_specs=[VMEM] * (2 + n_gate),
        out_shape=[
            jax.ShapeDtypeStruct(shape, jnp.float32),
            jax.ShapeDtypeStruct(shape, jnp.bfloat16),
        ]
        + [jax.ShapeDtypeStruct((n, block), jnp.float32)] * n_gate,
        compiler_params=pltpu.CompilerParams(vmem_limit_bytes=4 * MIB),
        cost_estimate=HEAVY,
    )(residual, gain[None, :], *pieces, *after)


def gate_up_kernel(n_ref, idx_ref, *refs):
    pieces = []
    for ref in refs[:n_ref]:
        pieces += [ref] if len(ref.shape) == 2 else [ref.at[i] for i in range(ref.shape[0])]
    n = len(pieces)
    wg_hbm, wu_hbm, weight_ref, gain_in = refs[n_ref : n_ref + 4]
    out_ref, gain_ref, x_ref, wg_ref, wu_ref, g_ref, u_ref, sq_ref, sems, wg_sems, wu_sems = refs[-11:]
    width = pieces[0].shape[1]
    rows = out_ref.shape[0]
    group = n // x_ref.shape[0]

    def load(i, j):
        at = pl.ds(pl.multiple_of(idx_ref[i * group + j] * width, width), width)
        to = pl.ds(j * width, width)
        return (
            pltpu.make_async_copy(pieces[0], x_ref.at[i, :, to], sems.at[i * group + j]),
            pltpu.make_async_copy(wg_hbm.at[at], wg_ref.at[i, to], wg_sems.at[i * group + j]),
            pltpu.make_async_copy(wu_hbm.at[at], wu_ref.at[i, to], wu_sems.at[i * group + j]),
        )

    for i in range(n):
        to = x_ref.at[i // group, :, pl.ds(i % group * width, width)]
        pltpu.make_async_copy(pieces[i], to, sems.at[i]).start()
        for copy in load(i // group, i % group)[1:]:
            copy.start()
    g_ref[...] = jnp.zeros_like(g_ref)
    u_ref[...] = jnp.zeros_like(u_ref)
    sq_ref[...] = jnp.zeros_like(sq_ref)
    gain_ref[...] = gain_in[...]

    @pl.loop(0, n // group)
    def _(i):
        for j in range(group):
            for copy in load(i, j):
                copy.wait()
        x = x_ref[i, :rows, :]
        if x_ref.shape[1] > rows:
            gain_ref[pl.ds(i, 1), :] = 1.0 / x_ref[i, rows:, :][0:1].astype(jnp.float32)
        g_ref[...] += jnp.dot(x, wg_ref[i], preferred_element_type=jnp.float32)
        u_ref[...] += jnp.dot(x, wu_ref[i], preferred_element_type=jnp.float32)
        hidden = x.astype(jnp.float32) * gain_ref[pl.ds(i, 1), :]
        sq_ref[...] += jnp.sum(hidden * hidden, axis=1, keepdims=True)

    inv = lax.rsqrt(sq_ref[...] / (n * width) + EPS)
    g = g_ref[...] * inv
    u = u_ref[...] * inv
    out_ref[...] = (g / (1.0 + jnp.exp(-g)) * u * weight_ref[...]).astype(jnp.bfloat16)


def gate_up(pieces, owners, w_gate, w_up, weight, gain):
    n = owners.shape[0]
    held, width = pieces[0].shape[-2:]
    rows = weight.shape[0]
    full, units = w_gate.shape
    group = 2 if width % 128 == 0 else 1
    groups, wide = n // group, group * width
    return pl.pallas_call(
        functools.partial(gate_up_kernel, len(pieces)),
        in_specs=[SMEM] + [ANY] * (len(pieces) + 2) + [VMEM] * 2,
        out_specs=[VMEM] * 2,
        out_shape=[
            jax.ShapeDtypeStruct((rows, units), jnp.bfloat16),
            jax.ShapeDtypeStruct((groups, wide), jnp.float32),
        ],
        scratch_shapes=[
            pltpu.VMEM((groups, held, wide), jnp.bfloat16),
            pltpu.VMEM((groups, wide, units), jnp.bfloat16),
            pltpu.VMEM((groups, wide, units), jnp.bfloat16),
            pltpu.VMEM((rows, units), jnp.float32),
            pltpu.VMEM((rows, units), jnp.float32),
            pltpu.VMEM((rows, 1), jnp.float32),
            pltpu.SemaphoreType.DMA((n,)),
            pltpu.SemaphoreType.DMA((n,)),
            pltpu.SemaphoreType.DMA((n,)),
        ],
        compiler_params=pltpu.CompilerParams(vmem_limit_bytes=30 * MIB),
        cost_estimate=HEAVY,
    )(owners, *pieces, in_hbm(w_gate), in_hbm(w_up), weight, gain.reshape(groups, wide))


def down_kernel(idx_ref, act_ref, w_ref, *refs):
    out_ref = refs[-1]
    m, _, width = out_ref.shape

    @pl.loop(0, m // 2)
    def _(j):
        even = idx_ref[2 * j] // 2 * 2
        swapped = idx_ref[2 * j] - even
        at = pl.ds(pl.multiple_of(even * width, 128), 2 * width)
        both = jnp.dot(act_ref[...], w_ref[:, at], preferred_element_type=jnp.float32)
        out_ref[2 * j + swapped] = both[:, :width].astype(jnp.bfloat16)
        out_ref[2 * j + 1 - swapped] = both[:, width:].astype(jnp.bfloat16)


def down(act, owners, w_down, width, after):
    rows, units = act.shape
    m = owners.shape[0]
    if width % 128 or m % 2:
        cut = [
            lax.dynamic_slice_in_dim(w_down, owners[j] * width, width, axis=1) for j in range(m)
        ]
        return jnp.stack(
            [jnp.dot(act, w, preferred_element_type=jnp.float32).astype(jnp.bfloat16) for w in cut]
        )
    return pl.pallas_call(
        down_kernel,
        in_specs=[SMEM, VMEM, VMEM] + [ANY] * len(after),
        out_specs=VMEM,
        out_shape=jax.ShapeDtypeStruct((m, rows, width), jnp.bfloat16),
        compiler_params=pltpu.CompilerParams(vmem_limit_bytes=8 * MIB),
        cost_estimate=HEAVY,
    )(owners, act, w_down, *after)


def combine_kernel(n, parts, near_ref, got_ref, *outs):
    size = near_ref.shape[1] // parts
    for p in range(parts):
        at = slice(p * size, (p + 1) * size)
        for d in range(n):
            both = near_ref[d, at, :].astype(jnp.float32) + got_ref[d, at, :].astype(jnp.float32)
            outs[p * n + d][...] = both.astype(outs[p * n + d].dtype)


def combine(near, got, parts):
    n, rows, width = near.shape
    outs = pl.pallas_call(
        functools.partial(combine_kernel, n, parts),
        in_specs=[VMEM] * 2,
        out_specs=[VMEM] * (n * parts),
        out_shape=[
            jax.ShapeDtypeStruct((rows // parts, width), jnp.bfloat16 if d else jnp.float32)
            for d in range(n)
        ]
        * parts,
        compiler_params=pltpu.CompilerParams(vmem_limit_bytes=12 * MIB),
        cost_estimate=HEAVY,
    )(near, got)
    return [outs[p * n : (p + 1) * n] for p in range(parts)]


def reduce_kernel(n, blocks, *refs):
    pieces, outs = refs[:n], refs[-blocks:]
    size = outs[0].shape[0]
    for b in range(blocks):
        at = slice(b * size, (b + 1) * size)
        total = pieces[0][at, :]
        for piece in pieces[1:]:
            total = total + piece[at, :].astype(jnp.float32)
        outs[b][...] = total.astype(outs[b].dtype)


def reduce(pieces, blocks, own, after):
    n = len(pieces)
    rows, width = pieces[0].shape
    return pl.pallas_call(
        functools.partial(reduce_kernel, n, blocks),
        in_specs=[VMEM] * n + [ANY] * len(after),
        out_specs=[VMEM] * blocks,
        out_shape=[
            jax.ShapeDtypeStruct((rows // blocks, width), jnp.bfloat16 if b or not own else jnp.float32)
            for b in range(blocks)
        ],
        compiler_params=pltpu.CompilerParams(vmem_limit_bytes=8 * MIB),
        cost_estimate=HEAVY,
    )(*pieces, *after)


def finish_kernel(counts, per, *refs):
    out_ref = refs[-1]
    chunks = len(counts)
    part = out_ref.shape[0] // (chunks * per)
    for c in range(chunks):
        pieces = refs[sum(counts[:c]) : sum(counts[: c + 1])]
        for p in range(per):
            at = slice(p * part, (p + 1) * part)
            total = pieces[0][at, :]
            for piece in pieces[1:]:
                total = total + piece[at, :].astype(jnp.float32)
            start = (p * chunks + c) * part
            out_ref[start : start + part, :] = total.astype(jnp.bfloat16)


def finish(terms, per):
    counts = [len(chunk) for chunk in terms]
    rows, width = terms[0][0].shape
    return pl.pallas_call(
        functools.partial(finish_kernel, counts, per),
        in_specs=[VMEM] * sum(counts),
        out_specs=VMEM,
        out_shape=jax.ShapeDtypeStruct((len(counts) * rows, width), jnp.bfloat16),
        compiler_params=pltpu.CompilerParams(vmem_limit_bytes=8 * MIB),
        cost_estimate=HEAVY,
    )(*[x for chunk in terms for x in chunk])


def attend_kernel(scale, chunk, len_ref, q_ref, c_ref, w_hbm, *refs):
    out_ref, w_ref, score_ref, prob_ref, lat_ref, sem = refs[-6:]
    step, steps = pl.program_id(0), pl.num_programs(0)
    group, heads, _ = q_ref.shape
    slots = c_ref.shape[2]
    _, latent_width, size = w_ref.shape
    load = pltpu.make_async_copy(w_hbm, w_ref, sem)

    @pl.when(step == 0)
    def _():
        load.start()

    places = lax.broadcasted_iota(jnp.int32, (heads, slots), 1)
    for r in range(group):
        scores = jnp.dot(q_ref[r], c_ref[r], preferred_element_type=jnp.float32) * scale
        live = len_ref[(chunk * steps + step) * group + r]
        score_ref[r * heads : (r + 1) * heads, :] = jnp.where(places < live, scores, -jnp.inf)
    scores = score_ref[...]
    exp_terms = jnp.exp(scores - jnp.max(scores, axis=1, keepdims=True))
    probs = exp_terms / jnp.sum(exp_terms, axis=1, keepdims=True)
    prob_ref[...] = probs.astype(jnp.bfloat16)
    for r in range(group):
        latent = lax.dot_general(
            prob_ref[r * heads : (r + 1) * heads, :],
            c_ref[r, :latent_width, :],
            (((1,), (1,)), ((), ())),
            preferred_element_type=jnp.float32,
        )
        at = pl.ds(pl.multiple_of((step * group + r) * heads, heads), heads)
        for k in range(latent_width // 128):
            lat_ref[k, at, :] = latent[:, k * 128 : (k + 1) * 128]

    @pl.when(step == steps - 1)
    def _():
        load.wait()
        for h in range(heads):
            at = pl.ds(h, out_ref.shape[0], stride=heads)
            latent = jnp.concatenate(
                [lat_ref[k, at, :] for k in range(latent_width // 128)], axis=1
            ).astype(jnp.bfloat16)
            out_ref[:, h * size : (h + 1) * size] = jnp.dot(
                latent, w_ref[h], preferred_element_type=jnp.float32
            ).astype(jnp.bfloat16)


def attend(queries, cache, lengths, w_uv, chunk, chunks, after):
    rows, heads, entries = queries.shape
    slots = cache.shape[1]
    _, latent_width, size = w_uv.shape
    group = 16
    steps = rows // chunks // group
    return pl.pallas_call(
        functools.partial(attend_kernel, (size + ROPE) ** (-0.5), chunk),
        grid_spec=pltpu.PrefetchScalarGridSpec(
            num_scalar_prefetch=1,
            grid=(steps,),
            in_specs=[
                pl.BlockSpec((group, heads, entries), lambda i, _: (chunk * steps + i, 0, 0)),
                pl.BlockSpec((group, entries, slots), lambda i, _: (chunk * steps + i, 0, 0)),
                ANY,
            ]
            + [ANY] * len(after),
            out_specs=pl.BlockSpec((steps * group, heads * size), lambda i, _: (0, 0)),
            scratch_shapes=[
                pltpu.VMEM(w_uv.shape, jnp.bfloat16),
                pltpu.VMEM((group * heads, slots), jnp.float32),
                pltpu.VMEM((group * heads, slots), jnp.bfloat16),
                pltpu.VMEM((latent_width // 128, steps * group * heads, 128), jnp.float32),
                pltpu.SemaphoreType.DMA,
            ],
        ),
        out_shape=jax.ShapeDtypeStruct((steps * group, heads * size), jnp.bfloat16),
        compiler_params=pltpu.CompilerParams(vmem_limit_bytes=20 * MIB),
        cost_estimate=HEAVY,
    )(
        lengths,
        in_hbm(queries),
        in_hbm(jnp.swapaxes(cache, 1, 2)),
        in_hbm(w_uv),
        *after,
    )


def shards(
    n_row,
    n_col,
    queries,
    cache,
    lengths,
    w_uv,
    w_out,
    residual_in,
    norm_gain,
    expert_ids,
    gate_vals,
    w_gate,
    w_up,
    w_down,
):
    side, row, col = lax.axis_index("side"), lax.axis_index("row"), lax.axis_index("col")
    block, width = residual_in.shape
    height = queries.shape[0]
    per = block // height
    chunks = 2
    part = height // chunks
    owners = jnp.stack(
        [(side ^ ds) * n_row + (row ^ d) for ds in range(2) for d in range(n_row)]
    ).astype(jnp.int32)
    places = (((owners // per) ^ col) * per + owners % per).astype(jnp.int32)

    chosen = expert_ids == owners[0]
    my_gate = jnp.sum(jnp.where(chosen, gate_vals, 0.0), axis=1)[None, :]
    gain = jnp.broadcast_to(norm_gain, (EXTRA, width))

    first = attend(queries, cache, lengths, w_uv, 0, chunks, [])
    second = attend(queries, cache, lengths, w_uv, 1, chunks, [first])
    gate_dev, up_dev, down_dev = w_gate[0], w_up[0], w_down[0]

    def over_col(pieces):
        return [pieces[0]] + [swap(pieces[d], "col", n_col, d) for d in range(1, n_col)]

    def over_row(pieces):
        return [pieces[0]] + [swap(pieces[d], "row", n_row, d) for d in range(1, n_row)]

    def other_core(x):
        return swap(x, "side", 2, 1)

    def experts(pieces, held, inverse_gain, parts, after):
        act, inverse_gain = gate_up(pieces, owners, gate_dev, up_dev, held, inverse_gain)
        far_rows = down(act, owners[n_row:], down_dev, width, [])
        near_rows = down(act, owners[:n_row], down_dev, width, after)
        return combine(near_rows, other_core(far_rows), parts), inverse_gain

    def stack_rows(x, after, estimate=HEAVY):
        return stack(over_row([x] * n_row), after, estimate).reshape(n_row, *x.shape)

    near_0 = stack_rows(first, [second], STACK)
    partial_0 = project(near_0, other_core(near_0), places, w_out, n_col, [], [])
    near_1 = stack_rows(second, partial_0[:1], STACK)
    hidden_0, scaled_0 = norm(residual_in, norm_gain, over_col(partial_0), 0, per, 0, [])
    partial_1 = project(near_1, other_core(near_1), places, w_out, n_col, [my_gate], [scaled_0])
    rows_0 = stack(over_col([scaled_0] * n_col) + [gain], partial_1[:1])
    hidden_1, scaled_1, gates = norm(
        residual_in, norm_gain, over_col(partial_1), 1, per, 1, [rows_0]
    )
    weight = gates.reshape(n_col, per, chunks, part)
    weight = [weight[:, :, c].reshape(-1, 1) for c in range(chunks)]
    near_0 = over_row([rows_0] * n_row)
    far_0 = [other_core(piece) for piece in near_0]
    no_gain = jnp.zeros((2 * n_row, width), jnp.float32)
    rows_1 = stack(over_col([scaled_1] * n_col), near_0[1:])
    far_own = other_core(rows_1)
    [both_0], inverse_gain = experts(near_0 + far_0, weight[0], no_gain, 1, [far_own])
    near_1 = stack(over_row([rows_1] * n_row)[1:], both_0[1:])
    near_1 = near_1.reshape(n_row - 1, *rows_1.shape)
    pieces = [rows_1, near_1, far_own, other_core(near_1)]
    both_1, _ = experts(pieces, hand_on(weight[1], [near_1]), inverse_gain, 2, [])
    total_0 = reduce(over_row(both_0), n_col, True, both_1[0][:1])
    terms_0 = [hidden_0, *over_col(total_0)]
    half = n_col // 2
    far_1 = reduce(over_row(both_1[1]), half, False, total_0[:1])
    last = [swap(far_1[d], "col", n_col, half + d) for d in range(half)]
    total_1 = reduce(over_row(both_1[0]), half, True, [far_1[0], *terms_0[2:]])
    first = [total_1[0]] + [swap(total_1[d], "col", n_col, d) for d in range(1, half)]
    [hidden_1] = reduce([hidden_1, *last], 1, True, total_1[:1])
    return finish([terms_0, [hidden_1, *first]], per)


def solution(mesh):
    placed = (
        P(("side", "row"), "col", None),
        P(("side", "row"), None, None),
        P(("side", "row")),
        P("col", None, None),
        P("col", ("side", "row")),
        P("col", ("side", "row")),
        P(("side", "row")),
        P("col", None),
        P("col", None),
        P(("side", "row"), None, "col"),
        P(("side", "row"), None, "col"),
        P(("side", "row"), "col", None),
    )
    return jax.shard_map(
        functools.partial(shards, mesh.shape["row"], mesh.shape["col"]),
        mesh=mesh,
        in_specs=placed,
        out_specs=P("col", ("side", "row")),
        check_vma=False,
    )
```

```python
import functools

import jax
import jax.numpy as jnp
from jax import lax
from jax.experimental import pallas as pl
from jax.experimental.pallas import tpu as pltpu
from jax.sharding import PartitionSpec as P

ROPE = 64
EPS = 1e-06
MIB = 1024 * 1024
EXTRA = 16
ANY = pl.BlockSpec(memory_space=pl.ANY)
VMEM = pl.BlockSpec(memory_space=pltpu.VMEM)
SMEM = pl.BlockSpec(memory_space=pltpu.SMEM)


def cost(us):
    return pl.CostEstimate(flops=int(us * 1e9), bytes_accessed=1024, transcendentals=0)


LIGHT, STACK, HEAVY = cost(0.001), cost(0.5), cost(100)


def in_hbm(x):
    return pltpu.with_memory_space_constraint(x, pltpu.HBM)


def swap(x, axis, count, d):
    return lax.ppermute(x, axis, [(i, i ^ d) for i in range(count)])


def stack_kernel(n, *refs):
    pieces, (out_ref, held_ref, in_sems, out_sems) = refs[:n], refs[-4:]
    loads, stores, start = [], [], 0
    for i in range(n):
        height = pieces[i].shape[0]
        at = held_ref.at[pl.ds(start, height)]
        loads.append(pltpu.make_async_copy(pieces[i], at, in_sems.at[i]))
        stores.append(
            pltpu.make_async_copy(at, out_ref.at[pl.ds(start, height)], out_sems.at[i])
        )
        start += height
    for load in loads:
        load.start()
    for load, store in zip(loads, stores):
        load.wait()
        store.start()
    for store in stores:
        store.wait()


def stack(pieces, after, estimate=HEAVY):
    n = len(pieces)
    shape = (sum(piece.shape[0] for piece in pieces), pieces[0].shape[1])
    return pl.pallas_call(
        functools.partial(stack_kernel, n),
        in_specs=[ANY] * (n + len(after)),
        out_specs=ANY,
        out_shape=jax.ShapeDtypeStruct(shape, pieces[0].dtype),
        scratch_shapes=[
            pltpu.VMEM(shape, pieces[0].dtype),
            pltpu.SemaphoreType.DMA((n,)),
            pltpu.SemaphoreType.DMA((n,)),
        ],
        compiler_params=pltpu.CompilerParams(vmem_limit_bytes=8 * MIB),
        cost_estimate=estimate,
    )(*pieces, *after)


def hand_on_kernel(x_ref, *refs):
    refs[-1][...] = x_ref[...]


def hand_on(x, after):
    return pl.pallas_call(
        hand_on_kernel,
        in_specs=[VMEM] + [ANY] * len(after),
        out_specs=VMEM,
        out_shape=jax.ShapeDtypeStruct(x.shape, x.dtype),
        compiler_params=pltpu.CompilerParams(vmem_limit_bytes=2 * MIB),
        cost_estimate=HEAVY,
    )(x, *after)


def project_kernel(blocks, n_gate, pos_ref, near_ref, far_ref, w_hbm, *refs):
    outs, (rows_ref, w_ref, acc_ref, sems, w_sems) = refs[-5 - blocks : -5], refs[-5:]
    half, height, full = near_ref.shape
    n = 2 * half
    pieces = [near_ref.at[i] for i in range(half)] + [far_ref.at[i] for i in range(half)]
    copies = [
        pltpu.make_async_copy(
            pieces[i],
            rows_ref.at[pl.ds(pl.multiple_of(pos_ref[i] * height, height), height)],
            sems.at[i],
        )
        for i in range(n)
    ]
    depth = min(512, full)

    def load(k):
        at = pl.ds(pl.multiple_of(k * depth, depth), depth)
        return pltpu.make_async_copy(w_hbm.at[at], w_ref.at[at], w_sems.at[k])

    for copy in copies:
        copy.start()
    for k in range(full // depth):
        load(k).start()
    acc_ref[...] = jnp.zeros_like(acc_ref)
    for copy in copies:
        copy.wait()

    @pl.loop(0, full // depth)
    def _(k):
        load(k).wait()
        at = pl.ds(pl.multiple_of(k * depth, depth), depth)
        acc_ref[...] += jnp.dot(
            rows_ref[:, at], w_ref[at, :], preferred_element_type=jnp.float32
        )

    size = acc_ref.shape[0] // blocks
    for d in range(blocks):
        outs[d][:size, :] = acc_ref[d * size : (d + 1) * size, :].astype(jnp.bfloat16)
    if n_gate:
        gate_ref = refs[0]
        rest, parts = gate_ref[...], []
        for _ in range(3):
            parts.append(rest.astype(jnp.bfloat16).astype(jnp.float32))
            rest = rest - parts[-1]
        parts.append(jnp.zeros((EXTRA - 3, rest.shape[1]), jnp.float32))
        parts = jnp.concatenate(parts, axis=0).astype(jnp.bfloat16)
        for d in range(blocks):
            outs[d][size:, :] = jnp.zeros((EXTRA, outs[d].shape[1]), jnp.bfloat16)
            outs[d][size:, : rest.shape[1]] = parts


def project(near, far, places, w_out, blocks, gate, after):
    half, height, full = near.shape
    n = 2 * half
    width = w_out.shape[1]
    rows = n * height
    held = rows // blocks + EXTRA * len(gate)
    return pl.pallas_call(
        functools.partial(project_kernel, blocks, len(gate)),
        in_specs=[SMEM, ANY, ANY, ANY] + [VMEM] * len(gate) + [ANY] * len(after),
        out_specs=[VMEM] * blocks,
        out_shape=[jax.ShapeDtypeStruct((held, width), jnp.bfloat16)] * blocks,
        scratch_shapes=[
            pltpu.VMEM((rows, full), jnp.bfloat16),
            pltpu.VMEM(w_out.shape, jnp.bfloat16),
            pltpu.VMEM((rows, width), jnp.float32),
            pltpu.SemaphoreType.DMA((n,)),
            pltpu.SemaphoreType.DMA((full // min(512, full),)),
        ],
        compiler_params=pltpu.CompilerParams(vmem_limit_bytes=18 * MIB),
        cost_estimate=HEAVY,
    )(places, near, far, in_hbm(w_out), *gate, *after)


def norm_kernel(chunk, per, n, n_gate, residual_ref, gain_ref, *refs):
    pieces, outs = refs[:n], refs[len(refs) - 2 - n_gate :]
    hidden_ref, scaled_ref = outs[:2]
    rows = hidden_ref.shape[0]
    part = rows // per
    height = residual_ref.shape[0] // per
    for p in range(per):
        to = slice(p * part, (p + 1) * part)
        start = p * height + chunk * part
        hidden = residual_ref[start : start + part, :].astype(jnp.float32)
        for piece in pieces:
            hidden = hidden + piece[to, :].astype(jnp.float32)
        hidden_ref[to, :] = hidden
        scaled_ref[to, :] = (hidden * gain_ref[...].astype(jnp.float32)).astype(jnp.bfloat16)
    if n_gate:
        for d in range(n):
            parts = pieces[d][rows:, : outs[2].shape[1]].astype(jnp.float32)
            outs[2][d : d + 1, :] = parts[0:1] + parts[1:2] + parts[2:3]


def norm(residual, gain, pieces, chunk, per, n_gate, after):
    n = len(pieces)
    block, width = residual.shape
    shape = (pieces[0].shape[0] - EXTRA * n_gate, width)
    return pl.pallas_call(
        functools.partial(norm_kernel, chunk, per, n, n_gate),
        in_specs=[VMEM] * (n + 2) + [ANY] * len(after),
        out_specs=[VMEM] * (2 + n_gate),
        out_shape=[
            jax.ShapeDtypeStruct(shape, jnp.float32),
            jax.ShapeDtypeStruct(shape, jnp.bfloat16),
        ]
        + [jax.ShapeDtypeStruct((n, block), jnp.float32)] * n_gate,
        compiler_params=pltpu.CompilerParams(vmem_limit_bytes=4 * MIB),
        cost_estimate=HEAVY,
    )(residual, gain[None, :], *pieces, *after)


def gate_up_kernel(n_ref, idx_ref, *refs):
    pieces = []
    for ref in refs[:n_ref]:
        pieces += [ref] if len(ref.shape) == 2 else [ref.at[i] for i in range(ref.shape[0])]
    n = len(pieces)
    wg_hbm, wu_hbm, weight_ref, gain_in = refs[n_ref : n_ref + 4]
    out_ref, gain_ref, x_ref, wg_ref, wu_ref, g_ref, u_ref, sq_ref, sems, wg_sems, wu_sems = refs[-11:]
    width = pieces[0].shape[1]
    rows = out_ref.shape[0]
    group = n // x_ref.shape[0]

    def load(i, j):
        at = pl.ds(pl.multiple_of(idx_ref[i * group + j] * width, width), width)
        to = pl.ds(j * width, width)
        return (
            pltpu.make_async_copy(pieces[0], x_ref.at[i, :, to], sems.at[i * group + j]),
            pltpu.make_async_copy(wg_hbm.at[at], wg_ref.at[i, to], wg_sems.at[i * group + j]),
            pltpu.make_async_copy(wu_hbm.at[at], wu_ref.at[i, to], wu_sems.at[i * group + j]),
        )

    for i in range(n):
        to = x_ref.at[i // group, :, pl.ds(i % group * width, width)]
        pltpu.make_async_copy(pieces[i], to, sems.at[i]).start()
        for copy in load(i // group, i % group)[1:]:
            copy.start()
    g_ref[...] = jnp.zeros_like(g_ref)
    u_ref[...] = jnp.zeros_like(u_ref)
    sq_ref[...] = jnp.zeros_like(sq_ref)
    gain_ref[...] = gain_in[...]

    @pl.loop(0, n // group)
    def _(i):
        for j in range(group):
            for copy in load(i, j):
                copy.wait()
        x = x_ref[i, :rows, :]
        if x_ref.shape[1] > rows:
            gain_ref[pl.ds(i, 1), :] = 1.0 / x_ref[i, rows:, :][0:1].astype(jnp.float32)
        g_ref[...] += jnp.dot(x, wg_ref[i], preferred_element_type=jnp.float32)
        u_ref[...] += jnp.dot(x, wu_ref[i], preferred_element_type=jnp.float32)
        hidden = x.astype(jnp.float32) * gain_ref[pl.ds(i, 1), :]
        sq_ref[...] += jnp.sum(hidden * hidden, axis=1, keepdims=True)

    inv = lax.rsqrt(sq_ref[...] / (n * width) + EPS)
    g = g_ref[...] * inv
    u = u_ref[...] * inv
    out_ref[...] = (g / (1.0 + jnp.exp(-g)) * u * weight_ref[...]).astype(jnp.bfloat16)


def gate_up(pieces, owners, w_gate, w_up, weight, gain):
    n = owners.shape[0]
    held, width = pieces[0].shape[-2:]
    rows = weight.shape[0]
    full, units = w_gate.shape
    group = 2 if width % 128 == 0 else 1
    groups, wide = n // group, group * width
    return pl.pallas_call(
        functools.partial(gate_up_kernel, len(pieces)),
        in_specs=[SMEM] + [ANY] * (len(pieces) + 2) + [VMEM] * 2,
        out_specs=[VMEM] * 2,
        out_shape=[
            jax.ShapeDtypeStruct((rows, units), jnp.bfloat16),
            jax.ShapeDtypeStruct((groups, wide), jnp.float32),
        ],
        scratch_shapes=[
            pltpu.VMEM((groups, held, wide), jnp.bfloat16),
            pltpu.VMEM((groups, wide, units), jnp.bfloat16),
            pltpu.VMEM((groups, wide, units), jnp.bfloat16),
            pltpu.VMEM((rows, units), jnp.float32),
            pltpu.VMEM((rows, units), jnp.float32),
            pltpu.VMEM((rows, 1), jnp.float32),
            pltpu.SemaphoreType.DMA((n,)),
            pltpu.SemaphoreType.DMA((n,)),
            pltpu.SemaphoreType.DMA((n,)),
        ],
        compiler_params=pltpu.CompilerParams(vmem_limit_bytes=30 * MIB),
        cost_estimate=HEAVY,
    )(owners, *pieces, in_hbm(w_gate), in_hbm(w_up), weight, gain.reshape(groups, wide))


def down_kernel(idx_ref, act_ref, w_ref, *refs):
    out_ref = refs[-1]
    m, _, width = out_ref.shape

    @pl.loop(0, m // 2)
    def _(j):
        even = idx_ref[2 * j] // 2 * 2
        swapped = idx_ref[2 * j] - even
        at = pl.ds(pl.multiple_of(even * width, 128), 2 * width)
        both = jnp.dot(act_ref[...], w_ref[:, at], preferred_element_type=jnp.float32)
        out_ref[2 * j + swapped] = both[:, :width].astype(jnp.bfloat16)
        out_ref[2 * j + 1 - swapped] = both[:, width:].astype(jnp.bfloat16)


def down(act, owners, w_down, width, after):
    rows, units = act.shape
    m = owners.shape[0]
    if width % 128 or m % 2:
        cut = [
            lax.dynamic_slice_in_dim(w_down, owners[j] * width, width, axis=1) for j in range(m)
        ]
        return jnp.stack(
            [jnp.dot(act, w, preferred_element_type=jnp.float32).astype(jnp.bfloat16) for w in cut]
        )
    return pl.pallas_call(
        down_kernel,
        in_specs=[SMEM, VMEM, VMEM] + [ANY] * len(after),
        out_specs=VMEM,
        out_shape=jax.ShapeDtypeStruct((m, rows, width), jnp.bfloat16),
        compiler_params=pltpu.CompilerParams(vmem_limit_bytes=8 * MIB),
        cost_estimate=HEAVY,
    )(owners, act, w_down, *after)


def combine_kernel(n, parts, near_ref, got_ref, *refs):
    outs = refs[-n * parts :]
    size = near_ref.shape[1] // parts
    for p in range(parts):
        at = slice(p * size, (p + 1) * size)
        for d in range(n):
            both = near_ref[d, at, :].astype(jnp.float32) + got_ref[d, at, :].astype(jnp.float32)
            outs[p * n + d][...] = both.astype(outs[p * n + d].dtype)


def combine(near, got, parts, after):
    n, rows, width = near.shape
    outs = pl.pallas_call(
        functools.partial(combine_kernel, n, parts),
        in_specs=[VMEM] * 2 + [ANY] * len(after),
        out_specs=[VMEM] * (n * parts),
        out_shape=[
            jax.ShapeDtypeStruct((rows // parts, width), jnp.bfloat16 if d else jnp.float32)
            for d in range(n)
        ]
        * parts,
        compiler_params=pltpu.CompilerParams(vmem_limit_bytes=12 * MIB),
        cost_estimate=HEAVY,
    )(near, got, *after)
    return [outs[p * n : (p + 1) * n] for p in range(parts)]


def reduce_kernel(n, blocks, *refs):
    pieces, outs = refs[:n], refs[-blocks:]
    size = outs[0].shape[0]
    for b in range(blocks):
        at = slice(b * size, (b + 1) * size)
        total = pieces[0][at, :]
        for piece in pieces[1:]:
            total = total + piece[at, :].astype(jnp.float32)
        outs[b][...] = total.astype(outs[b].dtype)


def reduce(pieces, blocks, own, after, estimate=HEAVY):
    n = len(pieces)
    rows, width = pieces[0].shape
    return pl.pallas_call(
        functools.partial(reduce_kernel, n, blocks),
        in_specs=[VMEM] * n + [ANY] * len(after),
        out_specs=[VMEM] * blocks,
        out_shape=[
            jax.ShapeDtypeStruct((rows // blocks, width), jnp.bfloat16 if b or not own else jnp.float32)
            for b in range(blocks)
        ],
        compiler_params=pltpu.CompilerParams(vmem_limit_bytes=8 * MIB),
        cost_estimate=estimate,
    )(*pieces, *after)


def finish_kernel(counts, per, *refs):
    out_ref = refs[-1]
    chunks = len(counts)
    part = out_ref.shape[0] // (chunks * per)
    for c in range(chunks):
        pieces = refs[sum(counts[:c]) : sum(counts[: c + 1])]
        for p in range(per):
            at = slice(p * part, (p + 1) * part)
            total = pieces[0][at, :]
            for piece in pieces[1:]:
                total = total + piece[at, :].astype(jnp.float32)
            start = (p * chunks + c) * part
            out_ref[start : start + part, :] = total.astype(jnp.bfloat16)


def finish(terms, per):
    counts = [len(chunk) for chunk in terms]
    rows, width = terms[0][0].shape
    return pl.pallas_call(
        functools.partial(finish_kernel, counts, per),
        in_specs=[VMEM] * sum(counts),
        out_specs=VMEM,
        out_shape=jax.ShapeDtypeStruct((len(counts) * rows, width), jnp.bfloat16),
        compiler_params=pltpu.CompilerParams(vmem_limit_bytes=8 * MIB),
        cost_estimate=HEAVY,
    )(*[x for chunk in terms for x in chunk])


def attend_kernel(scale, chunk, len_ref, q_ref, c_ref, w_hbm, *refs):
    out_ref, w_ref, score_ref, prob_ref, lat_ref, sem = refs[-6:]
    step, steps = pl.program_id(0), pl.num_programs(0)
    group, heads, _ = q_ref.shape
    slots = c_ref.shape[2]
    _, latent_width, size = w_ref.shape
    load = pltpu.make_async_copy(w_hbm, w_ref, sem)

    @pl.when(step == 0)
    def _():
        load.start()

    places = lax.broadcasted_iota(jnp.int32, (heads, slots), 1)
    for r in range(group):
        scores = jnp.dot(q_ref[r], c_ref[r], preferred_element_type=jnp.float32) * scale
        live = len_ref[(chunk * steps + step) * group + r]
        score_ref[r * heads : (r + 1) * heads, :] = jnp.where(places < live, scores, -jnp.inf)
    scores = score_ref[...]
    exp_terms = jnp.exp(scores - jnp.max(scores, axis=1, keepdims=True))
    probs = exp_terms / jnp.sum(exp_terms, axis=1, keepdims=True)
    prob_ref[...] = probs.astype(jnp.bfloat16)
    for r in range(group):
        latent = lax.dot_general(
            prob_ref[r * heads : (r + 1) * heads, :],
            c_ref[r, :latent_width, :],
            (((1,), (1,)), ((), ())),
            preferred_element_type=jnp.float32,
        )
        at = pl.ds(pl.multiple_of((step * group + r) * heads, heads), heads)
        for k in range(latent_width // 128):
            lat_ref[k, at, :] = latent[:, k * 128 : (k + 1) * 128]

    @pl.when(step == steps - 1)
    def _():
        load.wait()
        for h in range(heads):
            at = pl.ds(h, out_ref.shape[0], stride=heads)
            latent = jnp.concatenate(
                [lat_ref[k, at, :] for k in range(latent_width // 128)], axis=1
            ).astype(jnp.bfloat16)
            out_ref[:, h * size : (h + 1) * size] = jnp.dot(
                latent, w_ref[h], preferred_element_type=jnp.float32
            ).astype(jnp.bfloat16)


def attend(queries, cache, lengths, w_uv, chunk, chunks, after):
    rows, heads, entries = queries.shape
    slots = cache.shape[1]
    _, latent_width, size = w_uv.shape
    group = 16
    steps = rows // chunks // group
    return pl.pallas_call(
        functools.partial(attend_kernel, (size + ROPE) ** (-0.5), chunk),
        grid_spec=pltpu.PrefetchScalarGridSpec(
            num_scalar_prefetch=1,
            grid=(steps,),
            in_specs=[
                pl.BlockSpec((group, heads, entries), lambda i, _: (chunk * steps + i, 0, 0)),
                pl.BlockSpec((group, entries, slots), lambda i, _: (chunk * steps + i, 0, 0)),
                ANY,
            ]
            + [ANY] * len(after),
            out_specs=pl.BlockSpec((steps * group, heads * size), lambda i, _: (0, 0)),
            scratch_shapes=[
                pltpu.VMEM(w_uv.shape, jnp.bfloat16),
                pltpu.VMEM((group * heads, slots), jnp.float32),
                pltpu.VMEM((group * heads, slots), jnp.bfloat16),
                pltpu.VMEM((latent_width // 128, steps * group * heads, 128), jnp.float32),
                pltpu.SemaphoreType.DMA,
            ],
        ),
        out_shape=jax.ShapeDtypeStruct((steps * group, heads * size), jnp.bfloat16),
        compiler_params=pltpu.CompilerParams(vmem_limit_bytes=20 * MIB),
        cost_estimate=HEAVY,
    )(
        lengths,
        in_hbm(queries),
        in_hbm(jnp.swapaxes(cache, 1, 2)),
        in_hbm(w_uv),
        *after,
    )


def shards(
    n_row,
    n_col,
    queries,
    cache,
    lengths,
    w_uv,
    w_out,
    residual_in,
    norm_gain,
    expert_ids,
    gate_vals,
    w_gate,
    w_up,
    w_down,
):
    side, row, col = lax.axis_index("side"), lax.axis_index("row"), lax.axis_index("col")
    block, width = residual_in.shape
    height = queries.shape[0]
    per = block // height
    chunks = 2
    part = height // chunks
    owners = jnp.stack(
        [(side ^ ds) * n_row + (row ^ d) for ds in range(2) for d in range(n_row)]
    ).astype(jnp.int32)
    places = (((owners // per) ^ col) * per + owners % per).astype(jnp.int32)

    chosen = expert_ids == owners[0]
    my_gate = jnp.sum(jnp.where(chosen, gate_vals, 0.0), axis=1)[None, :]
    gain = jnp.broadcast_to(norm_gain, (EXTRA, width))

    first = attend(queries, cache, lengths, w_uv, 0, chunks, [])
    second = attend(queries, cache, lengths, w_uv, 1, chunks, [first])
    gate_dev, up_dev, down_dev = w_gate[0], w_up[0], w_down[0]

    def over_col(pieces):
        return [pieces[0]] + [swap(pieces[d], "col", n_col, d) for d in range(1, n_col)]

    def over_row(pieces):
        return [pieces[0]] + [swap(pieces[d], "row", n_row, d) for d in range(1, n_row)]

    def other_core(x):
        return swap(x, "side", 2, 1)

    def experts(pieces, held, inverse_gain, after):
        act, inverse_gain = gate_up(pieces, owners, gate_dev, up_dev, held, inverse_gain)
        far_rows = down(act, owners[n_row:], down_dev, width, [])
        near_rows = down(act, owners[:n_row], down_dev, width, after)
        return near_rows, other_core(far_rows), inverse_gain

    def stack_rows(x, after, estimate=HEAVY):
        return stack(over_row([x] * n_row), after, estimate).reshape(n_row, *x.shape)

    near_0 = stack_rows(first, [second], STACK)
    partial_0 = project(near_0, other_core(near_0), places, w_out, n_col, [], [])
    near_1 = stack_rows(second, partial_0[:1], STACK)
    hidden_0, scaled_0 = norm(residual_in, norm_gain, over_col(partial_0), 0, per, 0, [])
    partial_1 = project(near_1, other_core(near_1), places, w_out, n_col, [my_gate], [scaled_0])
    rows_0 = stack(over_col([scaled_0] * n_col) + [gain], partial_1[:1])
    hidden_1, scaled_1, gates = norm(
        residual_in, norm_gain, over_col(partial_1), 1, per, 1, [rows_0]
    )
    weight = gates.reshape(n_col, per, chunks, part)
    weight = [weight[:, :, c].reshape(-1, 1) for c in range(chunks)]
    near_0 = over_row([rows_0] * n_row)
    far_0 = [other_core(piece) for piece in near_0]
    no_gain = jnp.zeros((2 * n_row, width), jnp.float32)
    rows_1 = stack(over_col([scaled_1] * n_col), near_0[1:])
    far_own = other_core(rows_1)
    near_rows, got, inverse_gain = experts(near_0 + far_0, weight[0], no_gain, [far_own])
    [both_0] = combine(near_rows, got, 1, [])
    near_1 = stack(over_row([rows_1] * n_row)[1:], both_0[1:])
    near_1 = near_1.reshape(n_row - 1, *rows_1.shape)
    pieces = [rows_1, near_1, far_own, other_core(near_1)]
    near_rows, got, _ = experts(pieces, hand_on(weight[1], [near_1]), inverse_gain, [])
    total_0 = reduce(over_row(both_0), n_col, True, [near_rows], LIGHT)
    both_1 = combine(near_rows, got, 2, total_0[:1])
    terms_0 = [hidden_0, *over_col(total_0)]
    half = n_col // 2
    far_1 = reduce(over_row(both_1[1]), half, False, total_0[:1])
    last = [swap(far_1[d], "col", n_col, half + d) for d in range(half)]
    total_1 = reduce(over_row(both_1[0]), half, True, [far_1[0], *terms_0[2:]])
    first = [total_1[0]] + [swap(total_1[d], "col", n_col, d) for d in range(1, half)]
    [hidden_1] = reduce([hidden_1, *last], 1, True, total_1[:1])
    return finish([terms_0, [hidden_1, *first]], per)


def solution(mesh):
    placed = (
        P(("side", "row"), "col", None),
        P(("side", "row"), None, None),
        P(("side", "row")),
        P("col", None, None),
        P("col", ("side", "row")),
        P("col", ("side", "row")),
        P(("side", "row")),
        P("col", None),
        P("col", None),
        P(("side", "row"), None, "col"),
        P(("side", "row"), None, "col"),
        P(("side", "row"), "col", None),
    )
    return jax.shard_map(
        functools.partial(shards, mesh.shape["row"], mesh.shape["col"]),
        mesh=mesh,
        in_specs=placed,
        out_specs=P("col", ("side", "row")),
        check_vma=False,
    )
```

```python
import functools

import jax
import jax.numpy as jnp
from jax import lax
from jax.experimental import pallas as pl
from jax.experimental.pallas import tpu as pltpu
from jax.sharding import PartitionSpec as P

ROPE = 64
EPS = 1e-06
MIB = 1024 * 1024
EXTRA = 16
ANY = pl.BlockSpec(memory_space=pl.ANY)
VMEM = pl.BlockSpec(memory_space=pltpu.VMEM)
SMEM = pl.BlockSpec(memory_space=pltpu.SMEM)


def cost(us):
    return pl.CostEstimate(flops=int(us * 1e9), bytes_accessed=1024, transcendentals=0)


LIGHT, STACK, HEAVY = cost(0.001), cost(0.5), cost(100)


def in_hbm(x):
    return pltpu.with_memory_space_constraint(x, pltpu.HBM)


def swap(x, axis, count, d):
    return lax.ppermute(x, axis, [(i, i ^ d) for i in range(count)])


def stack_kernel(n, *refs):
    pieces, (out_ref, held_ref, in_sems, out_sems) = refs[:n], refs[-4:]
    loads, stores, start = [], [], 0
    for i in range(n):
        height = pieces[i].shape[0]
        at = held_ref.at[pl.ds(start, height)]
        loads.append(pltpu.make_async_copy(pieces[i], at, in_sems.at[i]))
        stores.append(
            pltpu.make_async_copy(at, out_ref.at[pl.ds(start, height)], out_sems.at[i])
        )
        start += height
    for load in loads:
        load.start()
    for load, store in zip(loads, stores):
        load.wait()
        store.start()
    for store in stores:
        store.wait()


def stack(pieces, after, estimate=HEAVY):
    n = len(pieces)
    shape = (sum(piece.shape[0] for piece in pieces), pieces[0].shape[1])
    return pl.pallas_call(
        functools.partial(stack_kernel, n),
        in_specs=[ANY] * (n + len(after)),
        out_specs=ANY,
        out_shape=jax.ShapeDtypeStruct(shape, pieces[0].dtype),
        scratch_shapes=[
            pltpu.VMEM(shape, pieces[0].dtype),
            pltpu.SemaphoreType.DMA((n,)),
            pltpu.SemaphoreType.DMA((n,)),
        ],
        compiler_params=pltpu.CompilerParams(vmem_limit_bytes=8 * MIB),
        cost_estimate=estimate,
    )(*pieces, *after)


def hand_on_kernel(x_ref, *refs):
    refs[-1][...] = x_ref[...]


def hand_on(x, after):
    return pl.pallas_call(
        hand_on_kernel,
        in_specs=[VMEM] + [ANY] * len(after),
        out_specs=VMEM,
        out_shape=jax.ShapeDtypeStruct(x.shape, x.dtype),
        compiler_params=pltpu.CompilerParams(vmem_limit_bytes=2 * MIB),
        cost_estimate=HEAVY,
    )(x, *after)


def project_kernel(blocks, n_gate, pos_ref, near_ref, far_ref, w_hbm, *refs):
    outs, (rows_ref, w_ref, acc_ref, sems, w_sems) = refs[-5 - blocks : -5], refs[-5:]
    half, height, full = near_ref.shape
    n = 2 * half
    pieces = [near_ref.at[i] for i in range(half)] + [far_ref.at[i] for i in range(half)]
    copies = [
        pltpu.make_async_copy(
            pieces[i],
            rows_ref.at[pl.ds(pl.multiple_of(pos_ref[i] * height, height), height)],
            sems.at[i],
        )
        for i in range(n)
    ]
    depth = min(512, full)

    def load(k):
        at = pl.ds(pl.multiple_of(k * depth, depth), depth)
        return pltpu.make_async_copy(w_hbm.at[at], w_ref.at[at], w_sems.at[k])

    for copy in copies:
        copy.start()
    for k in range(full // depth):
        load(k).start()
    acc_ref[...] = jnp.zeros_like(acc_ref)
    for copy in copies:
        copy.wait()

    @pl.loop(0, full // depth)
    def _(k):
        load(k).wait()
        at = pl.ds(pl.multiple_of(k * depth, depth), depth)
        acc_ref[...] += jnp.dot(
            rows_ref[:, at], w_ref[at, :], preferred_element_type=jnp.float32
        )

    size = acc_ref.shape[0] // blocks
    for d in range(blocks):
        outs[d][:size, :] = acc_ref[d * size : (d + 1) * size, :].astype(jnp.bfloat16)
    if n_gate:
        gate_ref = refs[0]
        rest, parts = gate_ref[...], []
        for _ in range(3):
            parts.append(rest.astype(jnp.bfloat16).astype(jnp.float32))
            rest = rest - parts[-1]
        parts.append(jnp.zeros((EXTRA - 3, rest.shape[1]), jnp.float32))
        parts = jnp.concatenate(parts, axis=0).astype(jnp.bfloat16)
        for d in range(blocks):
            outs[d][size:, :] = jnp.zeros((EXTRA, outs[d].shape[1]), jnp.bfloat16)
            outs[d][size:, : rest.shape[1]] = parts


def project(near, far, places, w_out, blocks, gate, after):
    half, height, full = near.shape
    n = 2 * half
    width = w_out.shape[1]
    rows = n * height
    held = rows // blocks + EXTRA * len(gate)
    return pl.pallas_call(
        functools.partial(project_kernel, blocks, len(gate)),
        in_specs=[SMEM, ANY, ANY, ANY] + [VMEM] * len(gate) + [ANY] * len(after),
        out_specs=[VMEM] * blocks,
        out_shape=[jax.ShapeDtypeStruct((held, width), jnp.bfloat16)] * blocks,
        scratch_shapes=[
            pltpu.VMEM((rows, full), jnp.bfloat16),
            pltpu.VMEM(w_out.shape, jnp.bfloat16),
            pltpu.VMEM((rows, width), jnp.float32),
            pltpu.SemaphoreType.DMA((n,)),
            pltpu.SemaphoreType.DMA((full // min(512, full),)),
        ],
        compiler_params=pltpu.CompilerParams(vmem_limit_bytes=18 * MIB),
        cost_estimate=HEAVY,
    )(places, near, far, in_hbm(w_out), *gate, *after)


def norm_kernel(chunk, per, n, n_gate, residual_ref, gain_ref, *refs):
    pieces, outs = refs[:n], refs[len(refs) - 2 - n_gate :]
    hidden_ref, scaled_ref = outs[:2]
    rows = hidden_ref.shape[0]
    part = rows // per
    height = residual_ref.shape[0] // per
    for p in range(per):
        to = slice(p * part, (p + 1) * part)
        start = p * height + chunk * part
        hidden = residual_ref[start : start + part, :].astype(jnp.float32)
        for piece in pieces:
            hidden = hidden + piece[to, :].astype(jnp.float32)
        hidden_ref[to, :] = hidden
        scaled_ref[to, :] = (hidden * gain_ref[...].astype(jnp.float32)).astype(jnp.bfloat16)
    if n_gate:
        for d in range(n):
            parts = pieces[d][rows:, : outs[2].shape[1]].astype(jnp.float32)
            outs[2][d : d + 1, :] = parts[0:1] + parts[1:2] + parts[2:3]


def norm(residual, gain, pieces, chunk, per, n_gate, after):
    n = len(pieces)
    block, width = residual.shape
    shape = (pieces[0].shape[0] - EXTRA * n_gate, width)
    return pl.pallas_call(
        functools.partial(norm_kernel, chunk, per, n, n_gate),
        in_specs=[VMEM] * (n + 2) + [ANY] * len(after),
        out_specs=[VMEM] * (2 + n_gate),
        out_shape=[
            jax.ShapeDtypeStruct(shape, jnp.float32),
            jax.ShapeDtypeStruct(shape, jnp.bfloat16),
        ]
        + [jax.ShapeDtypeStruct((n, block), jnp.float32)] * n_gate,
        compiler_params=pltpu.CompilerParams(vmem_limit_bytes=4 * MIB),
        cost_estimate=HEAVY,
    )(residual, gain[None, :], *pieces, *after)


def gate_up_kernel(n_ref, idx_ref, *refs):
    pieces = []
    for ref in refs[:n_ref]:
        pieces += [ref] if len(ref.shape) == 2 else [ref.at[i] for i in range(ref.shape[0])]
    n = len(pieces)
    wg_hbm, wu_hbm, weight_ref, gain_in = refs[n_ref : n_ref + 4]
    out_ref, gain_ref, x_ref, wg_ref, wu_ref, g_ref, u_ref, sq_ref, sems, wg_sems, wu_sems = refs[-11:]
    width = pieces[0].shape[1]
    rows = out_ref.shape[0]
    group = n // x_ref.shape[0]

    def load(i, j):
        at = pl.ds(pl.multiple_of(idx_ref[i * group + j] * width, width), width)
        to = pl.ds(j * width, width)
        return (
            pltpu.make_async_copy(pieces[0], x_ref.at[i, :, to], sems.at[i * group + j]),
            pltpu.make_async_copy(wg_hbm.at[at], wg_ref.at[i, to], wg_sems.at[i * group + j]),
            pltpu.make_async_copy(wu_hbm.at[at], wu_ref.at[i, to], wu_sems.at[i * group + j]),
        )

    for i in range(n):
        to = x_ref.at[i // group, :, pl.ds(i % group * width, width)]
        pltpu.make_async_copy(pieces[i], to, sems.at[i]).start()
        for copy in load(i // group, i % group)[1:]:
            copy.start()
    g_ref[...] = jnp.zeros_like(g_ref)
    u_ref[...] = jnp.zeros_like(u_ref)
    sq_ref[...] = jnp.zeros_like(sq_ref)
    gain_ref[...] = gain_in[...]

    @pl.loop(0, n // group)
    def _(i):
        for j in range(group):
            for copy in load(i, j):
                copy.wait()
        x = x_ref[i, :rows, :]
        if x_ref.shape[1] > rows:
            gain_ref[pl.ds(i, 1), :] = 1.0 / x_ref[i, rows:, :][0:1].astype(jnp.float32)
        g_ref[...] += jnp.dot(x, wg_ref[i], preferred_element_type=jnp.float32)
        u_ref[...] += jnp.dot(x, wu_ref[i], preferred_element_type=jnp.float32)
        hidden = x.astype(jnp.float32) * gain_ref[pl.ds(i, 1), :]
        sq_ref[...] += jnp.sum(hidden * hidden, axis=1, keepdims=True)

    inv = lax.rsqrt(sq_ref[...] / (n * width) + EPS)
    g = g_ref[...] * inv
    u = u_ref[...] * inv
    out_ref[...] = (g / (1.0 + jnp.exp(-g)) * u * weight_ref[...]).astype(jnp.bfloat16)


def gate_up(pieces, owners, w_gate, w_up, weight, gain):
    n = owners.shape[0]
    held, width = pieces[0].shape[-2:]
    rows = weight.shape[0]
    full, units = w_gate.shape
    group = 2 if width % 128 == 0 else 1
    groups, wide = n // group, group * width
    return pl.pallas_call(
        functools.partial(gate_up_kernel, len(pieces)),
        in_specs=[SMEM] + [ANY] * (len(pieces) + 2) + [VMEM] * 2,
        out_specs=[VMEM] * 2,
        out_shape=[
            jax.ShapeDtypeStruct((rows, units), jnp.bfloat16),
            jax.ShapeDtypeStruct((groups, wide), jnp.float32),
        ],
        scratch_shapes=[
            pltpu.VMEM((groups, held, wide), jnp.bfloat16),
            pltpu.VMEM((groups, wide, units), jnp.bfloat16),
            pltpu.VMEM((groups, wide, units), jnp.bfloat16),
            pltpu.VMEM((rows, units), jnp.float32),
            pltpu.VMEM((rows, units), jnp.float32),
            pltpu.VMEM((rows, 1), jnp.float32),
            pltpu.SemaphoreType.DMA((n,)),
            pltpu.SemaphoreType.DMA((n,)),
            pltpu.SemaphoreType.DMA((n,)),
        ],
        compiler_params=pltpu.CompilerParams(vmem_limit_bytes=30 * MIB),
        cost_estimate=HEAVY,
    )(owners, *pieces, in_hbm(w_gate), in_hbm(w_up), weight, gain.reshape(groups, wide))


def down_kernel(idx_ref, act_ref, w_ref, *refs):
    out_ref = refs[-1]
    m, _, width = out_ref.shape

    @pl.loop(0, m // 2)
    def _(j):
        even = idx_ref[2 * j] // 2 * 2
        swapped = idx_ref[2 * j] - even
        at = pl.ds(pl.multiple_of(even * width, 128), 2 * width)
        both = jnp.dot(act_ref[...], w_ref[:, at], preferred_element_type=jnp.float32)
        out_ref[2 * j + swapped] = both[:, :width].astype(jnp.bfloat16)
        out_ref[2 * j + 1 - swapped] = both[:, width:].astype(jnp.bfloat16)


def down(act, owners, w_down, width, after):
    rows, units = act.shape
    m = owners.shape[0]
    if width % 128 or m % 2:
        cut = [
            lax.dynamic_slice_in_dim(w_down, owners[j] * width, width, axis=1) for j in range(m)
        ]
        return jnp.stack(
            [jnp.dot(act, w, preferred_element_type=jnp.float32).astype(jnp.bfloat16) for w in cut]
        )
    return pl.pallas_call(
        down_kernel,
        in_specs=[SMEM, VMEM, VMEM] + [ANY] * len(after),
        out_specs=VMEM,
        out_shape=jax.ShapeDtypeStruct((m, rows, width), jnp.bfloat16),
        compiler_params=pltpu.CompilerParams(vmem_limit_bytes=8 * MIB),
        cost_estimate=HEAVY,
    )(owners, act, w_down, *after)


def combine_kernel(n, parts, near_ref, got_ref, *outs):
    size = near_ref.shape[1] // parts
    for p in range(parts):
        at = slice(p * size, (p + 1) * size)
        for d in range(n):
            both = near_ref[d, at, :].astype(jnp.float32) + got_ref[d, at, :].astype(jnp.float32)
            outs[p * n + d][...] = both.astype(outs[p * n + d].dtype)


def combine(near, got, parts):
    n, rows, width = near.shape
    outs = pl.pallas_call(
        functools.partial(combine_kernel, n, parts),
        in_specs=[VMEM] * 2,
        out_specs=[VMEM] * (n * parts),
        out_shape=[
            jax.ShapeDtypeStruct((rows // parts, width), jnp.bfloat16 if d else jnp.float32)
            for d in range(n)
        ]
        * parts,
        compiler_params=pltpu.CompilerParams(vmem_limit_bytes=12 * MIB),
        cost_estimate=HEAVY,
    )(near, got)
    return [outs[p * n : (p + 1) * n] for p in range(parts)]


def reduce_kernel(n, blocks, *refs):
    pieces, outs = refs[:n], refs[-blocks:]
    size = outs[0].shape[0]
    for b in range(blocks):
        at = slice(b * size, (b + 1) * size)
        total = pieces[0][at, :]
        for piece in pieces[1:]:
            total = total + piece[at, :].astype(jnp.float32)
        outs[b][...] = total.astype(outs[b].dtype)


def reduce(pieces, blocks, own, after):
    n = len(pieces)
    rows, width = pieces[0].shape
    return pl.pallas_call(
        functools.partial(reduce_kernel, n, blocks),
        in_specs=[VMEM] * n + [ANY] * len(after),
        out_specs=[VMEM] * blocks,
        out_shape=[
            jax.ShapeDtypeStruct((rows // blocks, width), jnp.bfloat16 if b or not own else jnp.float32)
            for b in range(blocks)
        ],
        compiler_params=pltpu.CompilerParams(vmem_limit_bytes=8 * MIB),
        cost_estimate=HEAVY,
    )(*pieces, *after)


def finish_kernel(counts, per, *refs):
    out_ref = refs[-1]
    chunks = len(counts)
    part = out_ref.shape[0] // (chunks * per)
    for c in range(chunks):
        pieces = refs[sum(counts[:c]) : sum(counts[: c + 1])]
        for p in range(per):
            at = slice(p * part, (p + 1) * part)
            total = pieces[0][at, :]
            for piece in pieces[1:]:
                total = total + piece[at, :].astype(jnp.float32)
            start = (p * chunks + c) * part
            out_ref[start : start + part, :] = total.astype(jnp.bfloat16)


def finish(terms, per):
    counts = [len(chunk) for chunk in terms]
    rows, width = terms[0][0].shape
    return pl.pallas_call(
        functools.partial(finish_kernel, counts, per),
        in_specs=[VMEM] * sum(counts),
        out_specs=VMEM,
        out_shape=jax.ShapeDtypeStruct((len(counts) * rows, width), jnp.bfloat16),
        compiler_params=pltpu.CompilerParams(vmem_limit_bytes=8 * MIB),
        cost_estimate=HEAVY,
    )(*[x for chunk in terms for x in chunk])


def attend_kernel(scale, chunk, len_ref, q_ref, c_ref, w_hbm, *refs):
    out_ref, w_ref, score_ref, prob_ref, lat_ref, sem = refs[-6:]
    step, steps = pl.program_id(0), pl.num_programs(0)
    group, heads, _ = q_ref.shape
    slots = c_ref.shape[2]
    _, latent_width, size = w_ref.shape
    load = pltpu.make_async_copy(w_hbm, w_ref, sem)

    @pl.when(step == 0)
    def _():
        load.start()

    places = lax.broadcasted_iota(jnp.int32, (heads, slots), 1)
    for r in range(group):
        scores = jnp.dot(q_ref[r], c_ref[r], preferred_element_type=jnp.float32) * scale
        live = len_ref[(chunk * steps + step) * group + r]
        score_ref[r * heads : (r + 1) * heads, :] = jnp.where(places < live, scores, -jnp.inf)
    scores = score_ref[...]
    exp_terms = jnp.exp(scores - jnp.max(scores, axis=1, keepdims=True))
    probs = exp_terms / jnp.sum(exp_terms, axis=1, keepdims=True)
    prob_ref[...] = probs.astype(jnp.bfloat16)
    for r in range(group):
        latent = lax.dot_general(
            prob_ref[r * heads : (r + 1) * heads, :],
            c_ref[r, :latent_width, :],
            (((1,), (1,)), ((), ())),
            preferred_element_type=jnp.float32,
        )
        at = pl.ds(pl.multiple_of((step * group + r) * heads, heads), heads)
        for k in range(latent_width // 128):
            lat_ref[k, at, :] = latent[:, k * 128 : (k + 1) * 128]

    @pl.when(step == steps - 1)
    def _():
        load.wait()
        for h in range(heads):
            at = pl.ds(h, out_ref.shape[0], stride=heads)
            latent = jnp.concatenate(
                [lat_ref[k, at, :] for k in range(latent_width // 128)], axis=1
            ).astype(jnp.bfloat16)
            out_ref[:, h * size : (h + 1) * size] = jnp.dot(
                latent, w_ref[h], preferred_element_type=jnp.float32
            ).astype(jnp.bfloat16)


def attend(queries, cache, lengths, w_uv, chunk, chunks, after):
    rows, heads, entries = queries.shape
    slots = cache.shape[1]
    _, latent_width, size = w_uv.shape
    group = 8
    steps = rows // chunks // group
    return pl.pallas_call(
        functools.partial(attend_kernel, (size + ROPE) ** (-0.5), chunk),
        grid_spec=pltpu.PrefetchScalarGridSpec(
            num_scalar_prefetch=1,
            grid=(steps,),
            in_specs=[
                pl.BlockSpec((group, heads, entries), lambda i, _: (chunk * steps + i, 0, 0)),
                pl.BlockSpec((group, entries, slots), lambda i, _: (chunk * steps + i, 0, 0)),
                ANY,
            ]
            + [ANY] * len(after),
            out_specs=pl.BlockSpec((steps * group, heads * size), lambda i, _: (0, 0)),
            scratch_shapes=[
                pltpu.VMEM(w_uv.shape, jnp.bfloat16),
                pltpu.VMEM((group * heads, slots), jnp.float32),
                pltpu.VMEM((group * heads, slots), jnp.bfloat16),
                pltpu.VMEM((latent_width // 128, steps * group * heads, 128), jnp.float32),
                pltpu.SemaphoreType.DMA,
            ],
        ),
        out_shape=jax.ShapeDtypeStruct((steps * group, heads * size), jnp.bfloat16),
        compiler_params=pltpu.CompilerParams(vmem_limit_bytes=20 * MIB),
        cost_estimate=HEAVY,
    )(
        lengths,
        in_hbm(queries),
        in_hbm(jnp.swapaxes(cache, 1, 2)),
        in_hbm(w_uv),
        *after,
    )


def shards(
    n_row,
    n_col,
    queries,
    cache,
    lengths,
    w_uv,
    w_out,
    residual_in,
    norm_gain,
    expert_ids,
    gate_vals,
    w_gate,
    w_up,
    w_down,
):
    side, row, col = lax.axis_index("side"), lax.axis_index("row"), lax.axis_index("col")
    block, width = residual_in.shape
    height = queries.shape[0]
    per = block // height
    chunks = 2
    part = height // chunks
    owners = jnp.stack(
        [(side ^ ds) * n_row + (row ^ d) for ds in range(2) for d in range(n_row)]
    ).astype(jnp.int32)
    places = (((owners // per) ^ col) * per + owners % per).astype(jnp.int32)

    chosen = expert_ids == owners[0]
    my_gate = jnp.sum(jnp.where(chosen, gate_vals, 0.0), axis=1)[None, :]
    gain = jnp.broadcast_to(norm_gain, (EXTRA, width))

    first = attend(queries, cache, lengths, w_uv, 0, chunks, [])
    second = attend(queries, cache, lengths, w_uv, 1, chunks, [first])
    gate_dev, up_dev, down_dev = w_gate[0], w_up[0], w_down[0]

    def over_col(pieces):
        return [pieces[0]] + [swap(pieces[d], "col", n_col, d) for d in range(1, n_col)]

    def over_row(pieces):
        return [pieces[0]] + [swap(pieces[d], "row", n_row, d) for d in range(1, n_row)]

    def other_core(x):
        return swap(x, "side", 2, 1)

    def experts(pieces, held, inverse_gain, parts, after):
        act, inverse_gain = gate_up(pieces, owners, gate_dev, up_dev, held, inverse_gain)
        far_rows = down(act, owners[n_row:], down_dev, width, [])
        near_rows = down(act, owners[:n_row], down_dev, width, after)
        return combine(near_rows, other_core(far_rows), parts), inverse_gain

    def stack_rows(x, after, estimate=HEAVY):
        return stack(over_row([x] * n_row), after, estimate).reshape(n_row, *x.shape)

    near_0 = stack_rows(first, [second], STACK)
    partial_0 = project(near_0, other_core(near_0), places, w_out, n_col, [], [])
    near_1 = stack_rows(second, partial_0[:1], STACK)
    hidden_0, scaled_0 = norm(residual_in, norm_gain, over_col(partial_0), 0, per, 0, [])
    partial_1 = project(near_1, other_core(near_1), places, w_out, n_col, [my_gate], [scaled_0])
    rows_0 = stack(over_col([scaled_0] * n_col) + [gain], partial_1[:1])
    hidden_1, scaled_1, gates = norm(
        residual_in, norm_gain, over_col(partial_1), 1, per, 1, [rows_0]
    )
    weight = gates.reshape(n_col, per, chunks, part)
    weight = [weight[:, :, c].reshape(-1, 1) for c in range(chunks)]
    near_0 = over_row([rows_0] * n_row)
    far_0 = [other_core(piece) for piece in near_0]
    no_gain = jnp.zeros((2 * n_row, width), jnp.float32)
    rows_1 = stack(over_col([scaled_1] * n_col), near_0[1:])
    far_own = other_core(rows_1)
    [both_0], inverse_gain = experts(near_0 + far_0, weight[0], no_gain, 1, [far_own])
    near_1 = stack(over_row([rows_1] * n_row)[1:], both_0[1:])
    near_1 = near_1.reshape(n_row - 1, *rows_1.shape)
    pieces = [rows_1, near_1, far_own, other_core(near_1)]
    both_1, _ = experts(pieces, hand_on(weight[1], [near_1]), inverse_gain, 2, [])
    total_0 = reduce(over_row(both_0), n_col, True, both_1[0][:1])
    terms_0 = [hidden_0, *over_col(total_0)]
    half = n_col // 2
    far_1 = reduce(over_row(both_1[1]), half, False, total_0[:1])
    last = [swap(far_1[d], "col", n_col, half + d) for d in range(half)]
    total_1 = reduce(over_row(both_1[0]), half, True, [far_1[0], *terms_0[2:]])
    first = [total_1[0]] + [swap(total_1[d], "col", n_col, d) for d in range(1, half)]
    [hidden_1] = reduce([hidden_1, *last], 1, True, total_1[:1])
    return finish([terms_0, [hidden_1, *first]], per)


def solution(mesh):
    placed = (
        P(("side", "row"), "col", None),
        P(("side", "row"), None, None),
        P(("side", "row")),
        P("col", None, None),
        P("col", ("side", "row")),
        P("col", ("side", "row")),
        P(("side", "row")),
        P("col", None),
        P("col", None),
        P(("side", "row"), None, "col"),
        P(("side", "row"), None, "col"),
        P(("side", "row"), "col", None),
    )
    return jax.shard_map(
        functools.partial(shards, mesh.shape["row"], mesh.shape["col"]),
        mesh=mesh,
        in_specs=placed,
        out_specs=P("col", ("side", "row")),
        check_vma=False,
    )
```
